512 devices in a mesh: pix: 16 (over y, x_lo, core), frame: 32 (over x_hi, z).
Axes of the slice: x: 4 (x_hi: 2, x_lo: 2; x = x_hi * 2 + x_lo), y: 4, z: 16, core: 2. Of those that a mesh axis runs over, the one named last changes fastest.
Arguments:
- frames: float32 [2048, 20480], P('frame', 'pix')
- start_basis: float32 [2048, 128], P('frame'), may hold values from -0.125 to 0.125
- picks: int32 [128], replicated, may hold values from 0 to 2047, as said below
- conv_in: bfloat16 [64, 9], replicated, may hold values from -2 to 2
- bias_in: float32 [64], replicated, may hold values from -3 to 3
- conv_out: bfloat16 [9, 64], replicated, may hold values from -0.25 to 0.25
- bias_out: float32 [1], replicated, may hold values from -1 to 1
Outputs:
- coeffs: float32 [2048, 128], P('frame')
- scores: float32 [128, 20480], P('frame', 'pix')
The draws below stay inside these ranges and needn't reach their ends.
Inputs may be any that keep to these rules, and one draw needn't show every extreme that they name: `picks`: indices may repeat; 0 and 2047 occur in every draw.
All inputs are finite; a program needn't handle non-finite values.
Results may differ from the reference program's by a relative error of at most 0.0013.
Values may be sent and summed in bfloat16 or wider, within the bound.
A program may use at most 64 MiB of HBM per device.

```python
import math
import jax
import jax.numpy as jnp
from jax import lax

W = 640
R = 128
HID = 64
ITERS = 2
H = 32
P_SIZE = 20480
F = 2048
SEL = 128


def draw_frames(key, part):
    key = jax.random.fold_in(key, 3)
    noise_key, pixel_key, frame_key = jax.random.split(key, 3)
    pixel_scale = jnp.exp(jax.random.uniform(pixel_key, (P_SIZE,), jnp.float32, math.log(0.1), 0.0))
    frame_scale = jnp.exp(jax.random.uniform(frame_key, (F, 1), jnp.float32, math.log(0.5), math.log(5.0)))
    noise = jnp.clip(jax.random.normal(noise_key, (F, P_SIZE), jnp.float32), -5.0, 5.0)
    return noise * pixel_scale[None, :] * frame_scale


def draw_picks(key, part):
    key = jax.random.fold_in(key, 7)
    first_key, second_key, third_key = jax.random.split(key, 3)
    chosen = jax.random.randint(first_key, (SEL,), 0, F)
    top_slot = jax.random.randint(second_key, (), 0, SEL)
    low_slot = (top_slot + 1 + jax.random.randint(third_key, (), 0, SEL - 1)) % SEL
    return chosen.at[top_slot].set(F - 1).at[low_slot].set(0)


def steps_of(own_key, extent, shards, least, high):
    def one(axis_at, shards_of):
        draws = jax.random.uniform(jax.random.fold_in(jax.random.fold_in(own_key, 6), axis_at), (shards_of,), jnp.float32, least / len(shards), high / len(shards))
        return jnp.repeat(jnp.exp(draws), extent[axis_at] // shards_of).reshape((-1,) + (1,) * (len(extent) - axis_at - 1))

    factor_of = one(*shards[0])
    for cut in shards[1:]:
        factor_of = factor_of * one(*cut)
    return factor_of


def scatter_about(stream_key, dims, deviation, limit, cuts=(), kind=jnp.bfloat16):
    factor_of = steps_of(stream_key, dims, cuts, -0.22, 0.18) if cuts else 1.0
    result = jax.random.normal(stream_key, dims, jnp.float32) * deviation * factor_of
    return jnp.minimum(jnp.maximum(result, -limit), limit).astype(kind)


def setup_inputs(seed: int = 0) -> dict:
    streams_of = jax.random.split(jax.random.key(seed), 8)
    return {
        "frames": draw_frames(jax.random.fold_in(streams_of[7], 71), 0),
        "start_basis": scatter_about(streams_of[1], (F, R), F ** -0.5, 0.125, ((0, 32),), jnp.float32),
        "picks": draw_picks(jax.random.fold_in(streams_of[7], 71), 0),
        "conv_in": scatter_about(streams_of[3], (HID, 9), 9 ** -0.5, 2.0),
        "bias_in": scatter_about(streams_of[4], (HID,), 0.5, 3.0, (), jnp.float32),
        "conv_out": scatter_about(streams_of[5], (9, HID), (9 * HID) ** -0.5, 0.25),
        "bias_out": jnp.clip(jax.random.uniform(streams_of[6], (1,), jnp.float32, -1.0, 1.0), -1.0, 1.0),
    }


threshold = 0.5

def orthonormal(block):
    gram = jnp.dot(block.T, block, precision=lax.Precision.HIGHEST)
    factor = jnp.linalg.cholesky(gram)
    return lax.linalg.triangular_solve(factor, block, left_side=False, lower=True, transpose_a=True)

def score_image(image, conv_in, bias_in, conv_out, bias_out):
    padded = jnp.pad(image.astype(jnp.float32), 1)
    hidden = jnp.zeros((HID, H, W), jnp.float32) + bias_in[:, None, None]
    for row_shift in range(3):
        for col_shift in range(3):
            tap_index = row_shift * 3 + col_shift
            weights = conv_in[:, tap_index].astype(jnp.float32)
            hidden = hidden + weights[:, None, None] * padded[None, row_shift:row_shift + H, col_shift:col_shift + W]
    hidden = lax.optimization_barrier(jnp.maximum(hidden, 0.0).astype(jnp.bfloat16)).astype(jnp.float32)
    widened = jnp.pad(hidden, ((0, 0), (1, 1), (1, 1)))
    total = jnp.zeros((H, W), jnp.float32) + bias_out[0]
    for row_shift in range(3):
        for col_shift in range(3):
            tap_index = row_shift * 3 + col_shift
            weights = conv_out[tap_index].astype(jnp.float32)
            total = total + jnp.einsum('c,chw->hw', weights, widened[:, row_shift:row_shift + H, col_shift:col_shift + W], precision=lax.Precision.HIGHEST)
    return total.reshape(-1)

def reference(frames, start_basis, picks, conv_in, bias_in, conv_out, bias_out):
    highest = lax.Precision.HIGHEST
    omega = start_basis
    coeffs = None
    ortho = None
    for step in range(ITERS):
        if step > 0:
            omega = coeffs
        basis = jnp.dot(frames.T, omega, precision=highest)
        ortho = orthonormal(basis)
        coeffs = jnp.dot(frames, ortho, precision=highest)
    chosen = frames[picks] - jnp.dot(coeffs[picks], ortho.T, precision=highest)
    shrunk = (jnp.sign(chosen) * jnp.maximum(jnp.abs(chosen) - threshold, 0.0)).astype(jnp.bfloat16)
    images = shrunk.reshape(SEL, H, W)
    scores = lax.map(lambda image: score_image(image, conv_in, bias_in, conv_out, bias_out), images)
    return (coeffs, scores)
```

```python
import jax
import jax.numpy as jnp
from jax import lax
from jax.experimental import pallas as pl
from jax.experimental.pallas import tpu as pltpu
from jax.sharding import PartitionSpec as P

MESH = pl.DeviceIdType.MESH
F32 = jnp.float32
BF16 = jnp.bfloat16

W = 640
RANK = 128
HID = 64
NZ = 16
NP = 16
FB = 64
PXH = 40
PX = 2 * PXH
FH = NZ * FB
THRESHOLD = 0.5


def dot(a, b):
    return lax.dot_general(
        a, b, (((1,), (0,)), ((), ())), precision=lax.Precision.HIGHEST, preferred_element_type=F32
    )


def dot_nt(a, b):
    return lax.dot_general(
        a, b, (((1,), (1,)), ((), ())), precision=lax.Precision.HIGHEST, preferred_element_type=F32
    )


def iota(shape, dim):
    return lax.broadcasted_iota(jnp.int32, shape, dim)


BLOCK = 32


def start_factor(work, gram):
    work[:, 0:RANK] = gram
    work[:, RANK : 2 * RANK] = (iota((RANK, RANK), 0) == iota((RANK, RANK), 1)).astype(F32)


def eliminate(work, result, first, last):
    tiles = BLOCK // 8
    row_in_tile = iota((8, 128), 0)

    def one(number, carry):
        left = [work[8 * t : 8 * t + 8, 0:RANK] for t in range(tiles)]
        right = [work[8 * t : 8 * t + 8, RANK:] for t in range(tiles)]
        columns = [
            [jnp.broadcast_to(left[t][:, m : m + 1], (8, 128)) for t in range(tiles)]
            for m in range(BLOCK)
        ]
        pivots = []
        for j in range(BLOCK):
            t0, r0 = j // 8, j % 8

            def row_of(tile):
                return jnp.broadcast_to(tile[r0 : r0 + 1, :], (8, 128))

            pivot = row_of(columns[j][t0])
            pivots.append(pivot)
            scale = 1.0 / pivot
            factors = [columns[j][t] * scale for t in range(tiles)]
            factors[t0] = jnp.where(row_in_tile > r0, factors[t0], 0.0)
            for m in range(j + 1, BLOCK):
                value = row_of(columns[m][t0])
                for t in range(t0, tiles):
                    columns[m][t] = columns[m][t] - factors[t] * value
            left_row, right_row = row_of(left[t0]), row_of(right[t0])
            for t in range(t0, tiles):
                left[t] = left[t] - factors[t] * left_row
                right[t] = right[t] - factors[t] * right_row
        for t in range(tiles):
            own = pivots[8 * t]
            for r in range(1, 8):
                own = jnp.where(row_in_tile == r, pivots[8 * t + r], own)
            scale = 1.0 / jnp.sqrt(own)
            left[t] = left[t] * scale
            right[t] = right[t] * scale
        left = jnp.concatenate(left, axis=0)
        right = jnp.concatenate(right, axis=0)
        result[pl.ds(pl.multiple_of(number * BLOCK, BLOCK), BLOCK), :] = right

        @pl.when(number < RANK // BLOCK - 1)
        def _():
            across = left.T[BLOCK:, :]
            rest = work[BLOCK:, 0:RANK] - dot(across, left)
            work[0 : RANK - BLOCK, 0:RANK] = pltpu.roll(rest, RANK - BLOCK, 1)
            work[0 : RANK - BLOCK, RANK:] = work[BLOCK:, RANK:] - dot(across, right)

        return carry

    lax.fori_loop(first, last, one, 0)


def push(src, dst, send, recv, device):
    pltpu.make_async_remote_copy(
        src_ref=src, dst_ref=dst, send_sem=send, recv_sem=recv,
        device_id={"frame": device[0], "pix": device[1]}, device_id_type=MESH,
    ).start()


def parts(x, count):
    out = []
    for _ in range(count):
        out.append(x.astype(BF16))
        x = x - out[-1].astype(F32)
    return out


def bdot(a, b):
    return jnp.dot(a, b, preferred_element_type=F32)


RING = (8, 7, 9, 6, 10, 5, 11, 4, 12, 3, 13, 2, 14, 1, 15)
EIGHTHS = (4, 2, 6, 5, 3, 7, 1)


def each(distances, send):
    for d in distances:
        send(d)


def drain(ref, sem):
    pltpu.make_async_copy(ref, ref, sem).wait()


def kernel(
    frames_hbm, basis0, picks_hbm, bias_in_hbm, conv_in, conv_out, bias_out,
    coeffs_out, scores_out,
    frames, picks, bias_in, t_buf, r_buf, om, at, an, sel_t, sel, xs, xr, ss, sr,
    s1, c1, t1, r1, k1, zy1, kg1, zg1, yz, yf, gf,
    s2, r2, k2, zy2, sg, rg, kg2, zg2, ft, fy,
    work, linv, slab, slabs, image, halo, taps, w1, w2, bias_wide,
    send, recv, load, arrive, came,
):
    group = lax.axis_index("frame")
    pix = lax.axis_index("pix")
    half = group // NZ
    z = group % NZ
    base = half * NZ
    q = pix // 2
    c = pix % 2
    fetch = pltpu.make_async_copy(frames_hbm, frames, load.at[0])
    fetch.start()
    fetch_picks = pltpu.make_async_copy(picks_hbm, picks, load.at[2])
    fetch_picks.start()
    fetch_bias = pltpu.make_async_copy(bias_in_hbm, bias_in, load.at[3])
    fetch_bias.start()

    across_group = (1 - half) * NZ + z
    partner = (across_group, pix)
    other_core = (group, 2 * q + 1 - c)
    wrap = lax.rem

    barrier = pltpu.get_barrier_semaphore()

    def greet(d):
        to = wrap(pix + d, NP)
        for frame, at_pix in ((base + wrap(z + d, NZ), pix), (group, to), (across_group, to)):
            pl.semaphore_signal(
                barrier, inc=1, device_id={"frame": frame, "pix": at_pix}, device_id_type=MESH
            )

    each(RING, greet)
    pl.semaphore_signal(
        barrier, inc=1, device_id={"frame": across_group, "pix": pix}, device_id_type=MESH
    )

    fetch.wait()
    both = jnp.concatenate([frames[:, 0:W], frames[:, W : 2 * W]], axis=0)
    for t in range(5):
        tile = both[:, 128 * t : 128 * t + 128].T
        for lo in range(128 * t, 128 * t + 128, 8):
            t_buf[lo // PXH, lo % PXH : lo % PXH + 8, :] = tile[lo - 128 * t : lo - 128 * t + 8, :]

    pl.semaphore_wait(barrier, 46)

    eighth = pl.multiple_of(q * 8, 8)

    def send_basis(d):
        push(
            basis0.at[pl.ds(eighth, 8)], om.at[z, q], send.at[0], recv.at[0],
            (base + wrap(z + d, NZ), pix),
        )

    def send_frames(d):
        to = wrap(z + d, NZ)
        push(t_buf.at[to], r_buf.at[z], send.at[1], came.at[z], (base + to, pix))

    each(RING, send_basis)
    each(RING[:9], send_frames)
    own_part = pltpu.make_async_copy(basis0.at[pl.ds(eighth, 8)], om.at[z, q], load.at[1])
    own_part.start()
    r_buf[z] = t_buf[z]
    own_part.wait()

    up = (iota((4 * HID, HID), 0) % HID == iota((4 * HID, HID), 1))
    wide = (iota((9, 72), 1) // 8 == iota((9, 72), 0))
    same = iota((4 * HID, 72), 0) // HID == iota((4 * HID, 72), 1) % 8
    spread = lax.dot_general(
        conv_in[...], wide.astype(BF16), (((0,), (0,)), ((), ())), preferred_element_type=F32
    ).astype(BF16)
    spread = jnp.dot(up.astype(BF16), spread, preferred_element_type=F32)
    w1[...] = jnp.where(same, spread, 0.0).astype(BF16)
    tall = (iota((72, 9), 0) // 8 == iota((72, 9), 1))
    over = (iota((HID, 4 * HID), 1) % HID == iota((HID, 4 * HID), 0))
    same = iota((72, 4 * HID), 1) // HID == iota((72, 4 * HID), 0) % 8
    spread = jnp.dot(tall.astype(BF16), conv_out[...], preferred_element_type=F32).astype(BF16)
    spread = jnp.dot(spread, over.astype(BF16), preferred_element_type=F32)
    w2[...] = jnp.where(same, spread, 0.0).astype(BF16)
    fetch_bias.wait()
    fetch_picks.wait()
    bias_wide[...] = dot_nt(up.astype(F32), jnp.broadcast_to(bias_in[...], (128, HID)))
    taps[...] = jnp.zeros_like(taps)

    drain(om.at[pl.ds(0, NZ - 1), 0], recv.at[0])

    def spread_basis(d):
        push(om.at[:, q], om.at[:, q], send.at[2], recv.at[2], (group, 2 * wrap(q + d, 8) + c))

    for d in EIGHTHS:
        spread_basis(d)
        each(RING[8 + EIGHTHS.index(d) : 9 + EIGHTHS.index(d)] if d != EIGHTHS[0] else (), send_frames)

    low = iota((PXH, 128), 1) < FB
    for k in (4, 3, 5, 2, 6, 1, 7, 0):
        m = wrap(z // 2 + k, NZ // 2)
        if k:
            drain(r_buf.at[2 * m], came.at[2 * m])
            drain(r_buf.at[2 * m + 1], came.at[2 * m + 1])
        else:
            other = 2 * m + 1 - z % 2
            drain(r_buf.at[other], came.at[other])
        first, second = r_buf[2 * m], r_buf[2 * m + 1]
        tile = jnp.concatenate(
            [
                jnp.where(low, first, pltpu.roll(second, FB, 1)),
                jnp.where(low, pltpu.roll(first, FB, 1), second),
            ],
            axis=0,
        )
        at[:, pl.ds(pl.multiple_of(128 * m, 128), 128)] = jnp.concatenate(parts(tile, 3), axis=0)

    def frames_times(x):
        out = bdot(at[...], jnp.concatenate(parts(x, 2), axis=1))
        out = out[:, 0:RANK] + out[:, RANK:]
        return out[0:PX] + (out[PX : 2 * PX] + out[2 * PX :])

    def rows_times(x):
        hi, lo = parts(x, 2)
        return bdot(an[...], jnp.concatenate([hi, hi, lo], axis=0))

    drain(om.at[:, pl.ds(0, 7)], recv.at[2])
    xs[0] = frames_times(om[...].reshape(FH, RANK))
    push(xs.at[0], xr.at[0], send.at[4], recv.at[4], partner)

    chosen_here = (iota((FH, 128), 0) + half * FH == picks[...]).astype(BF16)
    out = bdot(at[...], chosen_here)
    ss[...] = out[0:PX] + (out[PX : 2 * PX] + out[2 * PX :])
    push(ss, sr, send.at[3], recv.at[3], partner)
    for m in range(NZ // 2):
        tile = at[0 : 2 * PX, 128 * m : 128 * m + 128].astype(F32)
        tile = jnp.concatenate([tile, tile[0:PX]], axis=0)
        an[128 * m : 128 * m + 128, :] = tile.T.astype(BF16)
    drain(xr.at[0], recv.at[4])

    def to_pix(out, got, sem):
        def send_pix(d):
            to = wrap(pix + d, NP)
            push(out.at[to], got.at[pix], send.at[sem], recv.at[sem], (group, to))

        each(RING, send_pix)
        got[pix] = out[pix]

    def all_pix(buffer, sem):
        def send_pix(d):
            push(buffer.at[pix], buffer.at[pix], send.at[sem], recv.at[sem], (group, wrap(pix + d, NP)))

        each(RING, send_pix)

    def total(buffer, sem):
        drain(buffer.at[pl.ds(0, 15)], recv.at[sem])
        value = buffer[0]
        for s in range(1, 16):
            value = value + buffer[s]
        return value

    def tiles_to_z(packed, landed, sem):
        def send_z(d):
            to = wrap(z + d, NZ)
            push(packed.at[to % 8], landed.at[z], send.at[sem], recv.at[sem], (base + to, pix))

        each(RING, send_z)
        landed[z] = packed[z % 8]

    def same_to_z(packed, landed, sem):
        def send_z(d):
            push(packed, landed.at[z], send.at[sem], recv.at[sem], (base + wrap(z + d, NZ), pix))

        each(RING, send_z)
        landed[z] = packed[...]

    basis = xs[0] + xr[0]
    y = rows_times(basis)
    for qq in range(8):
        for cc in range(2):
            for k in range(8):
                row = FB * (8 * cc + k) + 8 * qq
                s1[cc, qq, k] = y[row : row + 8, :]
    gram = dot(basis.T, basis)
    for tile in range(NP):
        s1[tile % 2, tile // 2, 8] = gram[8 * tile : 8 * tile + 8, :]
    push(s1.at[1 - c], c1, send.at[5], recv.at[5], other_core)
    drain(sr, recv.at[3])
    sel_t[...] = ss[...] + sr[...]
    sel[...] = sel_t[...].T
    drain(c1, recv.at[5])
    for qq in range(8):
        t1[qq] = s1[c, qq] + c1[qq]

    def send_eighths(d):
        to = wrap(q + d, 8)
        push(t1.at[to], r1.at[q], send.at[21], recv.at[21], (group, 2 * to + c))

    each(EIGHTHS, send_eighths)
    r1[q] = t1[q]
    drain(r1.at[pl.ds(0, 7)], recv.at[21])
    value = r1[0]
    for s in range(1, 8):
        value = value + r1[s]
    k1[...] = value[0:8]
    kg1[...] = value[8]
    tiles_to_z(k1, zy1, 6)
    same_to_z(kg1, zg1, 17)
    yz[z % 8] = total(zy1, 6)
    for d in (4, -3, 3, -2, 2, -1, 1):
        push(
            yz.at[z % 8], yz.at[z % 8], send.at[7], recv.at[7],
            (base + wrap(z + (d + NZ) % NZ, NZ), pix),
        )
    gf[pix] = total(zg1, 17)
    all_pix(gf, 8)
    drain(yz.at[pl.ds(0, 7)], recv.at[7])
    ours, theirs = pl.ds(8 * c, 8), pl.ds(8 * (1 - c), 8)
    for d in EIGHTHS:
        push(
            yz, yf.at[ours, q], send.at[9], arrive.at[d], (group, 2 * wrap(q + d, 8) + c)
        )
    yf[ours, q] = yz[...]
    push(yf.at[ours, q], yf.at[ours, q], send.at[22], recv.at[22], other_core)
    drain(gf.at[pl.ds(0, NP - 1)], recv.at[8])
    start_factor(work, gf[...].reshape(RANK, RANK))
    eliminate(work, linv, 0, 2)
    for d in EIGHTHS:
        origin = wrap(q + 8 - d, 8)
        drain(yf.at[ours, origin], arrive.at[d])
        push(yf.at[ours, origin], yf.at[ours, origin], send.at[22], recv.at[22], other_core)
    eliminate(work, linv, 2, 3)
    drain(yf.at[theirs], recv.at[22])

    xs[1] = frames_times(yf[...].reshape(FH, RANK))
    push(xs.at[1], xr.at[1], send.at[10], recv.at[10], partner)
    eliminate(work, linv, 3, 4)
    drain(xr.at[1], recv.at[10])
    basis = dot_nt(xs[1] + xr[1], linv[...])
    across = basis.T
    sg[...] = dot(jnp.where(half == 0, across, sel[...]), basis).reshape(NP, 8, RANK)
    to_pix(sg, rg, 11)
    y = rows_times(basis)
    for owner in range(NP):
        for k in range(8):
            row = FB * (8 * (owner % 2) + k) + 8 * (owner // 2)
            s2[owner, k] = y[row : row + 8, :]
    kg2[...] = total(rg, 11)
    same_to_z(kg2, zg2, 13)
    to_pix(s2, r2, 12)
    place = half * NP + pix
    ft[place] = total(zg2, 13)

    def send_both(d):
        to = wrap(pix + d, NP)
        push(ft.at[place], ft.at[place], send.at[18], recv.at[18], (group, to))
        push(ft.at[place], ft.at[place], send.at[18], recv.at[18], (across_group, to))

    push(ft.at[place], ft.at[place], send.at[18], recv.at[18], partner)
    each(RING, send_both)
    k2[...] = total(r2, 12)
    tiles_to_z(k2, zy2, 19)
    drain(ft.at[pl.ds(0, 2 * NP - 1)], recv.at[18])
    start_factor(work, ft[0:NP].reshape(RANK, RANK))
    eliminate(work, linv, 0, 3)
    fy[pix] = total(zy2, 19)
    all_pix(fy, 20)
    eliminate(work, linv, 3, 4)

    own = dot_nt(ft[pl.ds(NP + 8 * half, 8)].reshape(FB, RANK), linv[...])
    ortho_t = dot(linv[...], across)
    chosen = sel[pl.ds(pl.multiple_of(FB * half, FB), FB), :] - dot(own, ortho_t)
    shrunk = jnp.where(
        chosen > THRESHOLD,
        chosen - THRESHOLD,
        jnp.where(chosen < -THRESHOLD, chosen + THRESHOLD, 0.0),
    )
    shrunk = shrunk.astype(BF16).astype(F32)
    shrunk = jnp.concatenate([shrunk, jnp.zeros((FB, 128 - PX), F32)], axis=1)
    for t in range(NZ):
        slab[t] = shrunk[4 * t : 4 * t + 4, :]

    def send_slab(d):
        to = wrap(z + d, NZ)
        push(slab.at[to], slabs.at[z], send.at[14], recv.at[14], (base + to, pix))

    each(RING, send_slab)
    slabs[z] = slab[z]
    drain(fy.at[pl.ds(0, NP - 1)], recv.at[20])
    upper = z >= 8
    mine = [jnp.where(upper, fy[2 * k + 1], fy[2 * k]) for k in range(8)]
    coeffs_out[...] = dot_nt(jnp.concatenate(mine, axis=0), linv[...])
    drain(slabs.at[pl.ds(0, NZ - 1)], recv.at[14])

    lane = iota((4, 128), 1)
    strips = []
    for row in range(2):
        tiles = [jnp.zeros((4, 128), F32) for _ in range(5)]
        for t in range(NZ):
            at_tile, shift = (PXH * t) // 128, (PXH * t) % 128
            piece = slabs[t]
            turn = (shift - PXH * row) % 128
            if turn:
                piece = pltpu.roll(piece, turn, 1)
            tiles[at_tile] = jnp.where((lane >= shift) & (lane < shift + PXH), piece, tiles[at_tile])
            if shift + PXH > 128:
                tiles[at_tile + 1] = jnp.where(lane < shift + PXH - 128, piece, tiles[at_tile + 1])
        strips.append(jnp.concatenate(tiles, axis=1))
    image[...] = jnp.concatenate(strips, axis=0)

    push(image, halo.at[0], send.at[15], recv.at[15], (group, wrap(pix + 1, NP)))
    push(image, halo.at[1], send.at[16], recv.at[16], (group, wrap(pix + NP - 1, NP)))
    drain(halo.at[0], recv.at[15])
    drain(halo.at[1], recv.at[16])
    first, last = pix == 0, pix == NP - 1
    above = jnp.where(first, 0.0, halo[0])
    below = jnp.where(last, 0.0, halo[1])
    here = image[...]
    rows = [above[0:4], above[4:8], here[0:4], here[4:8], below[0:4], below[4:8]]
    place_in_row = iota((4, W), 1)
    for b in range(3):
        for k, row in enumerate(rows):
            if b == 0:
                row = jnp.where(place_in_row == 0, 0.0, pltpu.roll(row, 1, 1))
            elif b == 2:
                row = jnp.where(place_in_row == W - 1, 0.0, pltpu.roll(row, W - 1, 1))
            for a in range(3):
                h = k - a
                if 0 <= h < 4:
                    tap = 3 * a + b
                    taps[8 * tap : 8 * tap + 4, W * h : W * h + W] = row
    bias = jnp.concatenate([bias_wide[...]] * 5, axis=1)
    layers = []
    for h in range(4):
        hidden = jnp.dot(
            w1[...], taps[:, W * h : W * h + W].astype(BF16), preferred_element_type=F32
        )
        hidden = jnp.maximum(hidden + bias, 0.0)
        if h == 0:
            hidden = jnp.where(first, 0.0, hidden)
        if h == 3:
            hidden = jnp.where(last, 0.0, hidden)
        layers.append(jnp.dot(w2[...], hidden.astype(BF16), preferred_element_type=F32))
    for r in range(2):
        summed = jnp.broadcast_to(bias_out[...], (4, W))
        for b in range(3):
            part = sum(layers[r + a][8 * (3 * a + b) : 8 * (3 * a + b) + 4, :] for a in range(3))
            if b == 0:
                part = jnp.where(place_in_row == 0, 0.0, pltpu.roll(part, 1, 1))
            elif b == 2:
                part = jnp.where(place_in_row == W - 1, 0.0, pltpu.roll(part, W - 1, 1))
            summed = summed + part
        scores_out[:, W * r : W * r + W] = summed

    drain(om.at[pl.ds(0, NZ - 1), 0], send.at[0])
    drain(t_buf.at[pl.ds(0, NZ - 1)], send.at[1])
    drain(om.at[:, pl.ds(0, 7)], send.at[2])
    drain(ss, send.at[3])
    drain(xs.at[0], send.at[4])
    drain(c1, send.at[5])
    drain(r1.at[pl.ds(0, 7)], send.at[21])
    drain(yf.at[theirs], send.at[22])
    drain(zy1.at[pl.ds(0, NZ - 1)], send.at[6])
    drain(yz.at[pl.ds(0, 7)], send.at[7])
    drain(gf.at[pl.ds(0, NP - 1)], send.at[8])
    drain(yf.at[pl.ds(0, 7)], send.at[9])
    drain(xs.at[1], send.at[10])
    drain(sg.at[pl.ds(0, NP - 1)], send.at[11])
    drain(s2.at[pl.ds(0, NP - 1)], send.at[12])
    drain(zg2.at[pl.ds(0, NZ - 1)], send.at[13])
    drain(zg1.at[pl.ds(0, NZ - 1)], send.at[17])
    drain(ft.at[pl.ds(0, 2 * NP - 1)], send.at[18])
    drain(zy2.at[pl.ds(0, NZ - 1)], send.at[19])
    drain(fy.at[pl.ds(0, NP - 1)], send.at[20])
    drain(slab.at[pl.ds(0, NZ - 1)], send.at[14])
    drain(image, send.at[15])
    drain(image, send.at[16])


def shards(frames, start_basis, picks, conv_in, bias_in, conv_out, bias_out):
    vmem = pltpu.VMEM
    scratch = [
        vmem((FB, 2 * W), F32),
        vmem((1, 128), jnp.int32),
        vmem((1, HID), F32),
        vmem((NZ, PXH, 128), F32),
        vmem((NZ, PXH, 128), F32),
        vmem((NZ, 8, 8, RANK), F32),
        vmem((3 * PX, FH), BF16),
        vmem((FH, 3 * PX), BF16),
        vmem((PX, 128), F32),
        vmem((128, PX), F32),
        vmem((2, PX, RANK), F32),
        vmem((2, PX, RANK), F32),
        vmem((PX, 128), F32),
        vmem((PX, 128), F32),
        vmem((2, 8, 9, 8, RANK), F32),
        vmem((8, 9, 8, RANK), F32),
        vmem((8, 9, 8, RANK), F32),
        vmem((8, 9, 8, RANK), F32),
        vmem((8, 8, RANK), F32),
        vmem((NZ, 8, RANK), F32),
        vmem((8, RANK), F32),
        vmem((NZ, 8, RANK), F32),
        vmem((8, 8, RANK), F32),
        vmem((NZ, 8, 8, RANK), F32),
        vmem((NP, 8, RANK), F32),
        vmem((NP, 8, 8, RANK), F32),
        vmem((NP, 8, 8, RANK), F32),
        vmem((8, 8, RANK), F32),
        vmem((NZ, 8, RANK), F32),
        vmem((NP, 8, RANK), F32),
        vmem((NP, 8, RANK), F32),
        vmem((8, RANK), F32),
        vmem((NZ, 8, RANK), F32),
        vmem((2 * NP, 8, RANK), F32),
        vmem((NP, 8, RANK), F32),
        vmem((RANK, 2 * RANK), F32),
        vmem((RANK, RANK), F32),
        vmem((NZ, 4, 128), F32),
        vmem((NZ, 4, 128), F32),
        vmem((8, W), F32),
        vmem((2, 8, W), F32),
        vmem((72, 4 * W), F32),
        vmem((4 * HID, 72), BF16),
        vmem((72, 4 * HID), BF16),
        vmem((4 * HID, 128), F32),
        pltpu.SemaphoreType.DMA((23,)),
        pltpu.SemaphoreType.DMA((23,)),
        pltpu.SemaphoreType.DMA((4,)),
        pltpu.SemaphoreType.DMA((8,)),
        pltpu.SemaphoreType.DMA((NZ,)),
    ]
    whole = pl.BlockSpec(memory_space=pltpu.VMEM)
    return pl.pallas_call(
        kernel,
        out_shape=(
            jax.ShapeDtypeStruct((FB, RANK), F32),
            jax.ShapeDtypeStruct((4, 2 * W), F32),
        ),
        in_specs=[pl.BlockSpec(memory_space=pltpu.HBM)] * 4 + [whole] * 3,
        out_specs=(whole, whole),
        scratch_shapes=scratch,
        compiler_params=pltpu.CompilerParams(
            collective_id=0, has_side_effects=True, vmem_limit_bytes=64 * 1024 * 1024
        ),
        cost_estimate=pl.CostEstimate(
            flops=1_500_000_000, bytes_accessed=1_000_000, transcendentals=0
        ),
    )(
        frames,
        start_basis,
        picks.reshape(1, 128),
        bias_in.reshape(1, HID),
        conv_in.T,
        conv_out,
        bias_out.reshape(1, 1),
    )


def solution(mesh):
    placed = (P("frame", "pix"), P("frame", None), P(), P(), P(), P(), P())
    return jax.shard_map(
        shards,
        mesh=mesh,
        in_specs=placed,
        out_specs=(P("frame", None), P("frame", "pix")),
        check_vma=False,
    )
```

```python
import jax
import jax.numpy as jnp
from jax import lax
from jax.experimental import pallas as pl
from jax.experimental.pallas import tpu as pltpu
from jax.sharding import PartitionSpec as P

MESH = pl.DeviceIdType.MESH
F32 = jnp.float32
BF16 = jnp.bfloat16

W = 640
RANK = 128
HID = 64
NZ = 16
NP = 16
FB = 64
PXH = 40
PX = 2 * PXH
FH = NZ * FB
THRESHOLD = 0.5


def dot(a, b):
    return lax.dot_general(
        a, b, (((1,), (0,)), ((), ())), precision=lax.Precision.HIGHEST, preferred_element_type=F32
    )


def dot_nt(a, b):
    return lax.dot_general(
        a, b, (((1,), (1,)), ((), ())), precision=lax.Precision.HIGHEST, preferred_element_type=F32
    )


def iota(shape, dim):
    return lax.broadcasted_iota(jnp.int32, shape, dim)


BLOCK = 32


def start_factor(work, gram):
    diagonal = iota((RANK, RANK), 0) == iota((RANK, RANK), 1)
    own = jnp.where(diagonal, gram, 0.0)
    by_row = 1.0 / jnp.sqrt(jnp.sum(own, axis=1, keepdims=True))
    by_column = 1.0 / jnp.sqrt(jnp.sum(own, axis=0, keepdims=True))
    work[:, 0:RANK] = gram * by_row * by_column
    work[:, RANK : 2 * RANK] = jnp.where(diagonal, by_column, 0.0)


def eliminate(work, result, first, last):
    tiles = BLOCK // 8
    row_in_tile = iota((8, 128), 0)

    def one(number, carry):
        left = [work[8 * t : 8 * t + 8, 0:RANK] for t in range(tiles)]
        right = [work[8 * t : 8 * t + 8, RANK:] for t in range(tiles)]
        columns = [
            [jnp.broadcast_to(left[t][:, m : m + 1], (8, 128)) for t in range(tiles)]
            for m in range(BLOCK)
        ]
        pivots = []
        for j in range(0, BLOCK, 2):
            t0, r0 = j // 8, j % 8

            def row_of(tile, r):
                return jnp.broadcast_to(tile[r : r + 1, :], (8, 128))

            one_, cross = row_of(columns[j][t0], r0), row_of(columns[j + 1][t0], r0)
            two = row_of(columns[j + 1][t0], r0 + 1)
            det = one_ * two - cross * cross
            over_one = 1.0 / one_
            over_two = one_ * (1.0 / det)
            link = cross * over_one
            pivots += [one_, det * over_one]
            first, second = {}, {}
            for t in range(t0, tiles):
                first[t] = columns[j][t] * over_one
                second[t] = (columns[j + 1][t] - link * columns[j][t]) * over_two
            first[t0] = jnp.where(row_in_tile > r0 + 1, first[t0], 0.0)
            second[t0] = jnp.where(row_in_tile > r0 + 1, second[t0], 0.0)
            for m in range(j + 2, BLOCK):
                upper = row_of(columns[m][t0], r0)
                lower = row_of(columns[m][t0], r0 + 1) - link * upper
                for t in range(t0, tiles):
                    columns[m][t] = columns[m][t] - (first[t] * upper + second[t] * lower)
            for side in (left, right):
                upper = row_of(side[t0], r0)
                lower = row_of(side[t0], r0 + 1) - link * upper
                for t in range(t0, tiles):
                    side[t] = side[t] - (first[t] * upper + second[t] * lower)
                side[t0] = jnp.where(row_in_tile == r0 + 1, lower, side[t0])
        for t in range(tiles):
            own = pivots[8 * t]
            for r in range(1, 8):
                own = jnp.where(row_in_tile == r, pivots[8 * t + r], own)
            scale = 1.0 / jnp.sqrt(own)
            left[t] = left[t] * scale
            right[t] = right[t] * scale
        left = jnp.concatenate(left, axis=0)
        right = jnp.concatenate(right, axis=0)
        result[pl.ds(pl.multiple_of(number * BLOCK, BLOCK), BLOCK), :] = right

        @pl.when(number < RANK // BLOCK - 1)
        def _():
            across = left.T[BLOCK:, :]
            rest = work[BLOCK:, 0:RANK] - dot(across, left)
            work[0 : RANK - BLOCK, 0:RANK] = pltpu.roll(rest, RANK - BLOCK, 1)
            work[0 : RANK - BLOCK, RANK:] = work[BLOCK:, RANK:] - dot(across, right)

        return carry

    lax.fori_loop(first, last, one, 0)


def push(src, dst, send, recv, device):
    pltpu.make_async_remote_copy(
        src_ref=src, dst_ref=dst, send_sem=send, recv_sem=recv,
        device_id={"frame": device[0], "pix": device[1]}, device_id_type=MESH,
    ).start()


def parts(x, count):
    out = []
    for _ in range(count):
        out.append(x.astype(BF16))
        x = x - out[-1].astype(F32)
    return out


def bdot(a, b):
    return jnp.dot(a, b, preferred_element_type=F32)


RING = (8, 7, 9, 6, 10, 5, 11, 4, 12, 3, 13, 2, 14, 1, 15)
EIGHTHS = (4, 2, 6, 5, 3, 7, 1)


def each(distances, send):
    for d in distances:
        send(d)


def drain(ref, sem):
    pltpu.make_async_copy(ref, ref, sem).wait()


def kernel(
    frames_hbm, basis0, picks_hbm, bias_in_hbm, conv_in, conv_out, bias_out,
    coeffs_out, scores_out,
    frames, picks, bias_in, t_buf, r_buf, om, at, an, sel_t, sel, xs, xr, ss, sr,
    s1, c1, t1, r1, k1, zy1, kg1, zg1, yz, yf, gf,
    s2, r2, k2, zy2, sg, rg, kg2, zg2, ft, fy,
    work, linv, slab, slabs, near, bs, selx, across_x, taps, w1, w2, bias_wide,
    send, recv, load, arrive, came,
):
    group = lax.axis_index("frame")
    pix = lax.axis_index("pix")
    half = group // NZ
    z = group % NZ
    base = half * NZ
    q = pix // 2
    c = pix % 2
    fetch = pltpu.make_async_copy(frames_hbm, frames, load.at[0])
    fetch.start()
    fetch_picks = pltpu.make_async_copy(picks_hbm, picks, load.at[2])
    fetch_picks.start()
    fetch_bias = pltpu.make_async_copy(bias_in_hbm, bias_in, load.at[3])
    fetch_bias.start()

    across_group = (1 - half) * NZ + z
    partner = (across_group, pix)
    other_core = (group, 2 * q + 1 - c)
    wrap = lax.rem

    barrier = pltpu.get_barrier_semaphore()

    def greet(d):
        to = wrap(pix + d, NP)
        for frame, at_pix in ((base + wrap(z + d, NZ), pix), (group, to), (across_group, to)):
            pl.semaphore_signal(
                barrier, inc=1, device_id={"frame": frame, "pix": at_pix}, device_id_type=MESH
            )

    each(RING, greet)
    pl.semaphore_signal(
        barrier, inc=1, device_id={"frame": across_group, "pix": pix}, device_id_type=MESH
    )

    fetch.wait()
    both = jnp.concatenate([frames[:, 0:W], frames[:, W : 2 * W]], axis=0)
    for t in range(5):
        tile = both[:, 128 * t : 128 * t + 128].T
        for lo in range(128 * t, 128 * t + 128, 8):
            t_buf[lo // PXH, lo % PXH : lo % PXH + 8, :] = tile[lo - 128 * t : lo - 128 * t + 8, :]

    pl.semaphore_wait(barrier, 46)

    eighth = pl.multiple_of(q * 8, 8)

    def send_basis(d):
        push(
            basis0.at[pl.ds(eighth, 8)], om.at[z, q], send.at[0], recv.at[0],
            (base + wrap(z + d, NZ), pix),
        )

    def send_frames(d):
        to = wrap(z + d, NZ)
        push(t_buf.at[to], r_buf.at[z], send.at[1], came.at[z], (base + to, pix))

    carries = c == z // 8

    @pl.when(carries)
    def _():
        each(RING, send_basis)

    each(RING[:9], send_frames)

    @pl.when(carries)
    def _():
        own_part = pltpu.make_async_copy(basis0.at[pl.ds(eighth, 8)], om.at[z, q], load.at[1])
        own_part.start()
        own_part.wait()

    r_buf[z] = t_buf[z]

    up = (iota((4 * HID, HID), 0) % HID == iota((4 * HID, HID), 1))
    wide = (iota((9, 72), 1) // 8 == iota((9, 72), 0))
    same = iota((4 * HID, 72), 0) // HID == iota((4 * HID, 72), 1) % 8
    spread = lax.dot_general(
        conv_in[...], wide.astype(BF16), (((0,), (0,)), ((), ())), preferred_element_type=F32
    ).astype(BF16)
    spread = jnp.dot(up.astype(BF16), spread, preferred_element_type=F32)
    w1[...] = jnp.where(same, spread, 0.0).astype(BF16)
    tall = (iota((72, 9), 0) // 8 == iota((72, 9), 1))
    over = (iota((HID, 4 * HID), 1) % HID == iota((HID, 4 * HID), 0))
    same = iota((72, 4 * HID), 1) // HID == iota((72, 4 * HID), 0) % 8
    spread = jnp.dot(tall.astype(BF16), conv_out[...], preferred_element_type=F32).astype(BF16)
    spread = jnp.dot(spread, over.astype(BF16), preferred_element_type=F32)
    w2[...] = jnp.where(same, spread, 0.0).astype(BF16)
    fetch_bias.wait()
    fetch_picks.wait()
    bias_wide[...] = dot_nt(up.astype(F32), jnp.broadcast_to(bias_in[...], (128, HID)))
    taps[...] = jnp.zeros_like(taps)

    @pl.when(carries)
    def _():
        drain(om.at[pl.ds(0, 7), 0], recv.at[0])

    @pl.when(c != z // 8)
    def _():
        drain(om.at[pl.ds(0, 8), 0], recv.at[0])

    lower_z = pl.ds(8 * c, 8)

    def spread_basis(d):
        push(
            om.at[lower_z, q], om.at[lower_z, q], send.at[2], recv.at[2], (group, wrap(pix + d, NP))
        )

    for n, d in enumerate(RING):
        spread_basis(d)
        each(RING[9 + n : 10 + n], send_frames)

    low = iota((PXH, 128), 1) < FB
    for k in (4, 3, 5, 2, 6, 1, 7, 0):
        m = wrap(z // 2 + k, NZ // 2)
        if k:
            drain(r_buf.at[2 * m], came.at[2 * m])
            drain(r_buf.at[2 * m + 1], came.at[2 * m + 1])
        else:
            other = 2 * m + 1 - z % 2
            drain(r_buf.at[other], came.at[other])
        first, second = r_buf[2 * m], r_buf[2 * m + 1]
        tile = jnp.concatenate(
            [
                jnp.where(low, first, pltpu.roll(second, FB, 1)),
                jnp.where(low, pltpu.roll(first, FB, 1), second),
            ],
            axis=0,
        )
        at[:, pl.ds(pl.multiple_of(128 * m, 128), 128)] = jnp.concatenate(parts(tile, 3), axis=0)

    def frames_times(x):
        out = bdot(at[...], jnp.concatenate(parts(x, 2), axis=1))
        out = out[:, 0:RANK] + out[:, RANK:]
        return out[0:PX] + (out[PX : 2 * PX] + out[2 * PX :])

    def rows_times(x):
        hi, lo = parts(x, 2)
        return bdot(an[...], jnp.concatenate([hi, hi, lo], axis=0))

    drain(om.at[pl.ds(0, 15)], recv.at[2])
    xs[0] = frames_times(om[...].reshape(FH, RANK))
    push(xs.at[0], xr.at[0], send.at[4], recv.at[4], partner)

    chosen_here = (iota((FH, 128), 0) + half * FH == picks[...]).astype(BF16)
    out = bdot(at[...], chosen_here)
    ss[...] = out[0:PX] + (out[PX : 2 * PX] + out[2 * PX :])
    push(ss, sr, send.at[3], recv.at[3], partner)
    for m in range(NZ // 2):
        tile = at[0 : 2 * PX, 128 * m : 128 * m + 128].astype(F32)
        tile = jnp.concatenate([tile, tile[0:PX]], axis=0)
        an[128 * m : 128 * m + 128, :] = tile.T.astype(BF16)
    drain(xr.at[0], recv.at[4])

    def to_pix(out, got, sem):
        def send_pix(d):
            to = wrap(pix + d, NP)
            push(out.at[to], got.at[pix], send.at[sem], recv.at[sem], (group, to))

        each(RING, send_pix)
        got[pix] = out[pix]

    def all_pix(buffer, sem):
        def send_pix(d):
            push(buffer.at[pix], buffer.at[pix], send.at[sem], recv.at[sem], (group, wrap(pix + d, NP)))

        each(RING, send_pix)

    def total(buffer, sem):
        drain(buffer.at[pl.ds(0, 15)], recv.at[sem])
        value = buffer[0]
        for s in range(1, 16):
            value = value + buffer[s]
        return value

    def tiles_to_z(packed, landed, sem):
        def send_z(d):
            to = wrap(z + d, NZ)
            push(packed.at[to % 8], landed.at[z], send.at[sem], recv.at[sem], (base + to, pix))

        each(RING, send_z)
        landed[z] = packed[z % 8]

    def same_to_z(packed, landed, sem):
        def send_z(d):
            push(packed, landed.at[z], send.at[sem], recv.at[sem], (base + wrap(z + d, NZ), pix))

        each(RING, send_z)
        landed[z] = packed[...]

    basis = xs[0] + xr[0]
    halves = parts(basis, 2)
    stacked = jnp.concatenate([halves[0], halves[0], halves[1]], axis=0)
    gram = dot(basis.T, basis)
    for tile in range(NP):
        s1[tile % 2, tile // 2, 8] = gram[8 * tile : 8 * tile + 8, :]

    def half_of_rows(which):
        y = bdot(an[pl.ds(pl.multiple_of(which * (FH // 2), FH // 2), FH // 2), :], stacked)
        for qq in range(8):
            for k in range(8):
                row = FB * k + 8 * qq
                s1[which, qq, k] = y[row : row + 8, :]

    half_of_rows(1 - c)
    push(s1.at[1 - c], c1, send.at[5], recv.at[5], other_core)
    half_of_rows(c)
    drain(c1, recv.at[5])

    def send_eighths(d):
        to = wrap(q + d, 8)
        t1[to] = s1[c, to] + c1[to]
        push(t1.at[to], r1.at[q], send.at[21], recv.at[21], (group, 2 * to + c))

    each(EIGHTHS, send_eighths)
    r1[q] = s1[c, q] + c1[q]
    drain(sr, recv.at[3])
    sel_t[...] = ss[...] + sr[...]
    sel[...] = sel_t[...].T
    push(sel_t, near.at[0], send.at[15], recv.at[15], (group, wrap(pix + 1, NP)))
    push(sel_t, near.at[1], send.at[16], recv.at[16], (group, wrap(pix + NP - 1, NP)))
    drain(r1.at[pl.ds(0, 7)], recv.at[21])
    value = r1[0]
    for s in range(1, 8):
        value = value + r1[s]
    k1[...] = value[0:8]
    kg1[...] = value[8]
    tiles_to_z(k1, zy1, 6)
    same_to_z(kg1, zg1, 17)
    yz[z % 8] = total(zy1, 6)
    for d in (4, -3, 3, -2, 2, -1, 1):
        push(
            yz.at[z % 8], yz.at[z % 8], send.at[7], recv.at[7],
            (base + wrap(z + (d + NZ) % NZ, NZ), pix),
        )
    gf[pix] = total(zg1, 17)
    all_pix(gf, 8)
    drain(yz.at[pl.ds(0, 7)], recv.at[7])
    ours, theirs = pl.ds(8 * c, 8), pl.ds(8 * (1 - c), 8)
    for d in EIGHTHS:
        push(
            yz, yf.at[ours, q], send.at[9], arrive.at[d], (group, 2 * wrap(q + d, 8) + c)
        )
    yf[ours, q] = yz[...]
    push(yf.at[ours, q], yf.at[ours, q], send.at[22], recv.at[22], other_core)
    drain(gf.at[pl.ds(0, NP - 1)], recv.at[8])
    start_factor(work, gf[...].reshape(RANK, RANK))
    eliminate(work, linv, 0, 2)
    for d in EIGHTHS:
        origin = wrap(q + 8 - d, 8)
        drain(yf.at[ours, origin], arrive.at[d])
        push(yf.at[ours, origin], yf.at[ours, origin], send.at[22], recv.at[22], other_core)
    eliminate(work, linv, 2, 3)
    drain(yf.at[theirs], recv.at[22])

    xs[1] = frames_times(yf[...].reshape(FH, RANK))
    push(xs.at[1], xr.at[1], send.at[10], recv.at[10], partner)
    eliminate(work, linv, 3, 4)
    drain(xr.at[1], recv.at[10])
    basis = dot_nt(xs[1] + xr[1], linv[...])
    across = basis.T
    sg[...] = dot(jnp.where(half == 0, across, sel[...]), basis).reshape(NP, 8, RANK)
    to_pix(sg, rg, 11)
    bs[...] = basis
    push(bs, near.at[2], send.at[23], recv.at[23], (group, wrap(pix + 1, NP)))
    push(bs, near.at[3], send.at[24], recv.at[24], (group, wrap(pix + NP - 1, NP)))
    y = rows_times(basis)
    for owner in range(NP):
        for k in range(8):
            row = FB * (8 * (owner % 2) + k) + 8 * (owner // 2)
            s2[owner, k] = y[row : row + 8, :]
    kg2[...] = total(rg, 11)
    same_to_z(kg2, zg2, 13)
    to_pix(s2, r2, 12)
    place = half * NP + pix
    ft[place] = total(zg2, 13)

    def send_both(d):
        to = wrap(pix + d, NP)
        push(ft.at[place], ft.at[place], send.at[18], recv.at[18], (group, to))
        push(ft.at[place], ft.at[place], send.at[18], recv.at[18], (across_group, to))

    push(ft.at[place], ft.at[place], send.at[18], recv.at[18], partner)
    each(RING, send_both)
    k2[...] = total(r2, 12)
    tiles_to_z(k2, zy2, 19)

    def with_near(own, above, below):
        gap = jnp.zeros((8, 128), F32)
        rows = [own, above[0:PXH], gap, above[PXH:], below, gap]
        return jnp.concatenate(rows, axis=0).T

    for k in range(4):
        drain(near.at[k], recv.at[(15, 16, 23, 24)[k]])
    selx[...] = with_near(sel_t[...], near[0], near[1])
    across_x[...] = with_near(bs[...], near[2], near[3])
    drain(ft.at[pl.ds(0, 2 * NP - 1)], recv.at[18])
    start_factor(work, ft[0:NP].reshape(RANK, RANK))
    eliminate(work, linv, 0, 3)
    fy[pix] = total(zy2, 19)
    all_pix(fy, 20)
    eliminate(work, linv, 3, 4)

    own = dot_nt(ft[pl.ds(NP + 8 * half, 8)].reshape(FB, RANK), linv[...])
    ortho_t = dot(linv[...], across_x[...])
    chosen = selx[pl.ds(pl.multiple_of(FB * half, FB), FB), :] - dot(own, ortho_t)
    shrunk = jnp.where(
        chosen > THRESHOLD,
        chosen - THRESHOLD,
        jnp.where(chosen < -THRESHOLD, chosen + THRESHOLD, 0.0),
    )
    shrunk = shrunk.astype(BF16).astype(F32)
    for t in range(NZ):
        slab[t] = shrunk[4 * t : 4 * t + 4, :]

    def send_slab(d):
        to = wrap(z + d, NZ)
        push(slab.at[to], slabs.at[z], send.at[14], recv.at[14], (base + to, pix))

    each(RING, send_slab)
    slabs[z] = slab[z]
    drain(fy.at[pl.ds(0, NP - 1)], recv.at[20])
    upper = z >= 8
    mine = [jnp.where(upper, fy[2 * k + 1], fy[2 * k]) for k in range(8)]
    coeffs_out[...] = dot_nt(jnp.concatenate(mine, axis=0), linv[...])
    drain(slabs.at[pl.ds(0, NZ - 1)], recv.at[14])

    lane = iota((4, 128), 1)
    first, last = pix == 0, pix == NP - 1
    rows = []
    for part, start in ((0, 80), (1, 0), (0, 0), (0, 40), (1, 40), (1, 80)):
        tiles = [jnp.zeros((4, 128), F32) for _ in range(5)]
        for t in range(NZ):
            at_tile, shift = (PXH * t) // 128, (PXH * t) % 128
            piece = slabs[t, :, 128 * part : 128 * part + 128]
            turn = (shift - start) % 128
            if turn:
                piece = pltpu.roll(piece, turn, 1)
            tiles[at_tile] = jnp.where((lane >= shift) & (lane < shift + PXH), piece, tiles[at_tile])
            if shift + PXH > 128:
                tiles[at_tile + 1] = jnp.where(lane < shift + PXH - 128, piece, tiles[at_tile + 1])
        row = jnp.concatenate(tiles, axis=1)
        if len(rows) < 2:
            row = jnp.where(first, 0.0, row)
        if len(rows) > 3:
            row = jnp.where(last, 0.0, row)
        rows.append(row)
    place_in_row = iota((4, W), 1)
    for b in range(3):
        for k, row in enumerate(rows):
            if b == 0:
                row = jnp.where(place_in_row == 0, 0.0, pltpu.roll(row, 1, 1))
            elif b == 2:
                row = jnp.where(place_in_row == W - 1, 0.0, pltpu.roll(row, W - 1, 1))
            for a in range(3):
                h = k - a
                if 0 <= h < 4:
                    tap = 3 * a + b
                    taps[8 * tap : 8 * tap + 4, W * h : W * h + W] = row
    bias = jnp.concatenate([bias_wide[...]] * 5, axis=1)
    layers = []
    for h in range(4):
        hidden = jnp.dot(
            w1[...], taps[:, W * h : W * h + W].astype(BF16), preferred_element_type=F32
        )
        hidden = jnp.maximum(hidden + bias, 0.0)
        if h == 0:
            hidden = jnp.where(first, 0.0, hidden)
        if h == 3:
            hidden = jnp.where(last, 0.0, hidden)
        layers.append(jnp.dot(w2[...], hidden.astype(BF16), preferred_element_type=F32))
    for r in range(2):
        summed = jnp.broadcast_to(bias_out[...], (4, W))
        for b in range(3):
            part = sum(layers[r + a][8 * (3 * a + b) : 8 * (3 * a + b) + 4, :] for a in range(3))
            if b == 0:
                part = jnp.where(place_in_row == 0, 0.0, pltpu.roll(part, 1, 1))
            elif b == 2:
                part = jnp.where(place_in_row == W - 1, 0.0, pltpu.roll(part, W - 1, 1))
            summed = summed + part
        scores_out[:, W * r : W * r + W] = summed

    @pl.when(carries)
    def _():
        drain(om.at[pl.ds(0, NZ - 1), 0], send.at[0])

    drain(t_buf.at[pl.ds(0, NZ - 1)], send.at[1])
    drain(om.at[pl.ds(0, 15)], send.at[2])
    drain(ss, send.at[3])
    drain(xs.at[0], send.at[4])
    drain(c1, send.at[5])
    drain(r1.at[pl.ds(0, 7)], send.at[21])
    drain(yf.at[theirs], send.at[22])
    drain(zy1.at[pl.ds(0, NZ - 1)], send.at[6])
    drain(yz.at[pl.ds(0, 7)], send.at[7])
    drain(gf.at[pl.ds(0, NP - 1)], send.at[8])
    drain(yf.at[pl.ds(0, 7)], send.at[9])
    drain(xs.at[1], send.at[10])
    drain(sg.at[pl.ds(0, NP - 1)], send.at[11])
    drain(s2.at[pl.ds(0, NP - 1)], send.at[12])
    drain(zg2.at[pl.ds(0, NZ - 1)], send.at[13])
    drain(zg1.at[pl.ds(0, NZ - 1)], send.at[17])
    drain(ft.at[pl.ds(0, 2 * NP - 1)], send.at[18])
    drain(zy2.at[pl.ds(0, NZ - 1)], send.at[19])
    drain(fy.at[pl.ds(0, NP - 1)], send.at[20])
    drain(slab.at[pl.ds(0, NZ - 1)], send.at[14])
    for sem in (15, 16, 23, 24):
        drain(bs, send.at[sem])


def shards(frames, start_basis, picks, conv_in, bias_in, conv_out, bias_out):
    vmem = pltpu.VMEM
    scratch = [
        vmem((FB, 2 * W), F32),
        vmem((1, 128), jnp.int32),
        vmem((1, HID), F32),
        vmem((NZ, PXH, 128), F32),
        vmem((NZ, PXH, 128), F32),
        vmem((NZ, 8, 8, RANK), F32),
        vmem((3 * PX, FH), BF16),
        vmem((FH, 3 * PX), BF16),
        vmem((PX, 128), F32),
        vmem((128, PX), F32),
        vmem((2, PX, RANK), F32),
        vmem((2, PX, RANK), F32),
        vmem((PX, 128), F32),
        vmem((PX, 128), F32),
        vmem((2, 8, 9, 8, RANK), F32),
        vmem((8, 9, 8, RANK), F32),
        vmem((8, 9, 8, RANK), F32),
        vmem((8, 9, 8, RANK), F32),
        vmem((8, 8, RANK), F32),
        vmem((NZ, 8, RANK), F32),
        vmem((8, RANK), F32),
        vmem((NZ, 8, RANK), F32),
        vmem((8, 8, RANK), F32),
        vmem((NZ, 8, 8, RANK), F32),
        vmem((NP, 8, RANK), F32),
        vmem((NP, 8, 8, RANK), F32),
        vmem((NP, 8, 8, RANK), F32),
        vmem((8, 8, RANK), F32),
        vmem((NZ, 8, RANK), F32),
        vmem((NP, 8, RANK), F32),
        vmem((NP, 8, RANK), F32),
        vmem((8, RANK), F32),
        vmem((NZ, 8, RANK), F32),
        vmem((2 * NP, 8, RANK), F32),
        vmem((NP, 8, RANK), F32),
        vmem((RANK, 2 * RANK), F32),
        vmem((RANK, RANK), F32),
        vmem((NZ, 4, 256), F32),
        vmem((NZ, 4, 256), F32),
        vmem((4, PX, 128), F32),
        vmem((PX, RANK), F32),
        vmem((128, 256), F32),
        vmem((RANK, 256), F32),
        vmem((72, 4 * W), F32),
        vmem((4 * HID, 72), BF16),
        vmem((72, 4 * HID), BF16),
        vmem((4 * HID, 128), F32),
        pltpu.SemaphoreType.DMA((25,)),
        pltpu.SemaphoreType.DMA((25,)),
        pltpu.SemaphoreType.DMA((4,)),
        pltpu.SemaphoreType.DMA((8,)),
        pltpu.SemaphoreType.DMA((NZ,)),
    ]
    whole = pl.BlockSpec(memory_space=pltpu.VMEM)
    return pl.pallas_call(
        kernel,
        out_shape=(
            jax.ShapeDtypeStruct((FB, RANK), F32),
            jax.ShapeDtypeStruct((4, 2 * W), F32),
        ),
        in_specs=[pl.BlockSpec(memory_space=pltpu.HBM)] * 4 + [whole] * 3,
        out_specs=(whole, whole),
        scratch_shapes=scratch,
        compiler_params=pltpu.CompilerParams(
            collective_id=0, has_side_effects=True, vmem_limit_bytes=64 * 1024 * 1024
        ),
        cost_estimate=pl.CostEstimate(
            flops=1_500_000_000, bytes_accessed=1_000_000, transcendentals=0
        ),
    )(
        frames,
        start_basis,
        picks.reshape(1, 128),
        bias_in.reshape(1, HID),
        conv_in.T,
        conv_out,
        bias_out.reshape(1, 1),
    )


def solution(mesh):
    placed = (P("frame", "pix"), P("frame", None), P(), P(), P(), P(), P())
    return jax.shard_map(
        shards,
        mesh=mesh,
        in_specs=placed,
        out_specs=(P("frame", None), P("frame", "pix")),
        check_vma=False,
    )
```

```python
import jax
import jax.numpy as jnp
from jax import lax
from jax.experimental import pallas as pl
from jax.experimental.pallas import tpu as pltpu
from jax.sharding import PartitionSpec as P

MESH = pl.DeviceIdType.MESH
F32 = jnp.float32
BF16 = jnp.bfloat16

W = 640
RANK = 128
HID = 64
NZ = 16
NP = 16
FB = 64
PXH = 40
PX = 2 * PXH
FH = NZ * FB
THRESHOLD = 0.5


def dot(a, b):
    return lax.dot_general(
        a, b, (((1,), (0,)), ((), ())), precision=lax.Precision.HIGHEST, preferred_element_type=F32
    )


def dot_nt(a, b):
    return lax.dot_general(
        a, b, (((1,), (1,)), ((), ())), precision=lax.Precision.HIGHEST, preferred_element_type=F32
    )


def iota(shape, dim):
    return lax.broadcasted_iota(jnp.int32, shape, dim)


BLOCK = 32


def start_factor(work, gram):
    diagonal = iota((RANK, RANK), 0) == iota((RANK, RANK), 1)
    own = jnp.where(diagonal, gram, 0.0)
    by_row = 1.0 / jnp.sqrt(jnp.sum(own, axis=1, keepdims=True))
    by_column = 1.0 / jnp.sqrt(jnp.sum(own, axis=0, keepdims=True))
    work[:, 0:RANK] = gram * by_row * by_column
    work[:, RANK : 2 * RANK] = jnp.where(diagonal, by_column, 0.0)


def eliminate(work, result, first, last):
    tiles = BLOCK // 8
    row_in_tile = iota((8, 128), 0)

    def one(number, carry):
        left = [work[8 * t : 8 * t + 8, 0:RANK] for t in range(tiles)]
        right = [work[8 * t : 8 * t + 8, RANK:] for t in range(tiles)]
        columns = [
            [jnp.broadcast_to(left[t][:, m : m + 1], (8, 128)) for t in range(tiles)]
            for m in range(BLOCK)
        ]
        pivots = []
        for j in range(0, BLOCK, 2):
            t0, r0 = j // 8, j % 8

            def row_of(tile, r):
                return jnp.broadcast_to(tile[r : r + 1, :], (8, 128))

            one_, cross = row_of(columns[j][t0], r0), row_of(columns[j + 1][t0], r0)
            two = row_of(columns[j + 1][t0], r0 + 1)
            det = one_ * two - cross * cross
            over_one = 1.0 / one_
            over_two = one_ * (1.0 / det)
            link = cross * over_one
            pivots += [one_, det * over_one]
            first, second = {}, {}
            for t in range(t0, tiles):
                first[t] = columns[j][t] * over_one
                second[t] = (columns[j + 1][t] - link * columns[j][t]) * over_two
            first[t0] = jnp.where(row_in_tile > r0 + 1, first[t0], 0.0)
            second[t0] = jnp.where(row_in_tile > r0 + 1, second[t0], 0.0)
            for m in range(j + 2, BLOCK):
                upper = row_of(columns[m][t0], r0)
                lower = row_of(columns[m][t0], r0 + 1) - link * upper
                for t in range(t0, tiles):
                    columns[m][t] = columns[m][t] - (first[t] * upper + second[t] * lower)
            for side in (left, right):
                upper = row_of(side[t0], r0)
                lower = row_of(side[t0], r0 + 1) - link * upper
                for t in range(t0, tiles):
                    side[t] = side[t] - (first[t] * upper + second[t] * lower)
                side[t0] = jnp.where(row_in_tile == r0 + 1, lower, side[t0])
        for t in range(tiles):
            own = pivots[8 * t]
            for r in range(1, 8):
                own = jnp.where(row_in_tile == r, pivots[8 * t + r], own)
            scale = 1.0 / jnp.sqrt(own)
            left[t] = left[t] * scale
            right[t] = right[t] * scale
        left = jnp.concatenate(left, axis=0)
        right = jnp.concatenate(right, axis=0)
        result[pl.ds(pl.multiple_of(number * BLOCK, BLOCK), BLOCK), :] = right

        @pl.when(number < RANK // BLOCK - 1)
        def _():
            across = left.T[BLOCK:, :]
            rest = work[BLOCK:, 0:RANK] - dot(across, left)
            work[0 : RANK - BLOCK, 0:RANK] = pltpu.roll(rest, RANK - BLOCK, 1)
            work[0 : RANK - BLOCK, RANK:] = work[BLOCK:, RANK:] - dot(across, right)

        return carry

    lax.fori_loop(first, last, one, 0)


def push(src, dst, send, recv, device):
    pltpu.make_async_remote_copy(
        src_ref=src, dst_ref=dst, send_sem=send, recv_sem=recv,
        device_id={"frame": device[0], "pix": device[1]}, device_id_type=MESH,
    ).start()


def parts(x, count):
    out = []
    for _ in range(count):
        out.append(x.astype(BF16))
        x = x - out[-1].astype(F32)
    return out


def bdot(a, b):
    return jnp.dot(a, b, preferred_element_type=F32)


RING = (8, 7, 9, 6, 10, 5, 11, 4, 12, 3, 13, 2, 14, 1, 15)
EIGHTHS = (4, 2, 6, 5, 3, 7, 1)


def each(distances, send):
    for d in distances:
        send(d)


def drain(ref, sem):
    pltpu.make_async_copy(ref, ref, sem).wait()


def kernel(
    frames_hbm, basis0, picks_hbm, bias_in_hbm, conv_in_hbm, conv_out_hbm, bias_out_hbm,
    coeffs_out, scores_out,
    frames, picks, bias_in, conv_in, conv_out, bias_out, t_buf, r_buf, om, at, an, sel_t, sel, xs, xr, ss, sr,
    s1, g1, c1, cg1, t1, r1, k1, zy1, kg1, zg1, yz, yf, gf,
    s2, r2, k2, zy2, sg, rg, kg2, zg2, ft, fy,
    work, linv, slab, slabs, near, bs, selx, across_x, taps, w1, w2, bias_wide,
    send, recv, load, arrive, came,
):
    group = lax.axis_index("frame")
    pix = lax.axis_index("pix")
    half = group // NZ
    z = group % NZ
    base = half * NZ
    q = pix // 2
    c = pix % 2
    fetch = pltpu.make_async_copy(frames_hbm, frames, load.at[0])
    fetch.start()
    small = [
        pltpu.make_async_copy(src, dst, load.at[2 + n])
        for n, (src, dst) in enumerate(
            (
                (picks_hbm, picks),
                (bias_in_hbm, bias_in),
                (conv_in_hbm, conv_in),
                (conv_out_hbm, conv_out),
                (bias_out_hbm, bias_out),
            )
        )
    ]
    for copy in small:
        copy.start()

    across_group = (1 - half) * NZ + z
    partner = (across_group, pix)
    other_core = (group, 2 * q + 1 - c)
    wrap = lax.rem

    barrier = pltpu.get_barrier_semaphore()

    def greet(d):
        to = wrap(pix + d, NP)
        for frame, at_pix in ((base + wrap(z + d, NZ), pix), (group, to), (across_group, to)):
            pl.semaphore_signal(
                barrier, inc=1, device_id={"frame": frame, "pix": at_pix}, device_id_type=MESH
            )

    each(RING, greet)
    pl.semaphore_signal(
        barrier, inc=1, device_id={"frame": across_group, "pix": pix}, device_id_type=MESH
    )

    fetch.wait()
    both = jnp.concatenate([frames[:, 0:W], frames[:, W : 2 * W]], axis=0)
    for t in range(5):
        tile = both[:, 128 * t : 128 * t + 128].T
        for lo in range(128 * t, 128 * t + 128, 8):
            t_buf[lo // PXH, lo % PXH : lo % PXH + 8, :] = tile[lo - 128 * t : lo - 128 * t + 8, :]

    pl.semaphore_wait(barrier, 46)

    eighth = pl.multiple_of(q * 8, 8)

    def send_basis(d):
        push(
            basis0.at[pl.ds(eighth, 8)], om.at[z, q], send.at[0], recv.at[0],
            (base + wrap(z + d, NZ), pix),
        )

    def send_frames(d):
        to = wrap(z + d, NZ)
        push(t_buf.at[to], r_buf.at[z], send.at[1], came.at[z], (base + to, pix))

    carries = c == z // 8

    @pl.when(carries)
    def _():
        each(RING, send_basis)

    each(RING[:4], send_frames)

    @pl.when(carries)
    def _():
        own_part = pltpu.make_async_copy(basis0.at[pl.ds(eighth, 8)], om.at[z, q], load.at[1])
        own_part.start()
        own_part.wait()

    r_buf[z] = t_buf[z]

    for copy in small:
        copy.wait()
    up = (iota((4 * HID, HID), 0) % HID == iota((4 * HID, HID), 1))
    wide = (iota((9, 72), 1) // 8 == iota((9, 72), 0))
    same = iota((4 * HID, 72), 0) // HID == iota((4 * HID, 72), 1) % 8
    spread = lax.dot_general(
        conv_in[...], wide.astype(BF16), (((0,), (0,)), ((), ())), preferred_element_type=F32
    ).astype(BF16)
    spread = jnp.dot(up.astype(BF16), spread, preferred_element_type=F32)
    w1[...] = jnp.where(same, spread, 0.0).astype(BF16)
    tall = (iota((72, 9), 0) // 8 == iota((72, 9), 1))
    over = (iota((HID, 4 * HID), 1) % HID == iota((HID, 4 * HID), 0))
    same = iota((72, 4 * HID), 1) // HID == iota((72, 4 * HID), 0) % 8
    spread = jnp.dot(tall.astype(BF16), conv_out[...], preferred_element_type=F32).astype(BF16)
    spread = jnp.dot(spread, over.astype(BF16), preferred_element_type=F32)
    w2[...] = jnp.where(same, spread, 0.0).astype(BF16)
    bias_wide[...] = dot_nt(up.astype(F32), jnp.broadcast_to(bias_in[...], (128, HID)))
    taps[...] = jnp.zeros_like(taps)

    @pl.when(carries)
    def _():
        drain(om.at[pl.ds(0, 7), 0], recv.at[0])

    @pl.when(c != z // 8)
    def _():
        drain(om.at[pl.ds(0, 8), 0], recv.at[0])

    lower_z = pl.ds(8 * c, 8)

    def spread_basis(d):
        push(
            om.at[lower_z, q], om.at[lower_z, q], send.at[2], recv.at[2], (group, wrap(pix + d, NP))
        )

    for n, d in enumerate(RING):
        spread_basis(d)
        each(RING[4 + n : 5 + n], send_frames)

    low = iota((PXH, 128), 1) < FB
    for k in (4, 3, 5, 2, 6, 1, 7, 0):
        m = wrap(z // 2 + k, NZ // 2)
        if k:
            drain(r_buf.at[2 * m], came.at[2 * m])
            drain(r_buf.at[2 * m + 1], came.at[2 * m + 1])
        else:
            other = 2 * m + 1 - z % 2
            drain(r_buf.at[other], came.at[other])
        first, second = r_buf[2 * m], r_buf[2 * m + 1]
        tile = jnp.concatenate(
            [
                jnp.where(low, first, pltpu.roll(second, FB, 1)),
                jnp.where(low, pltpu.roll(first, FB, 1), second),
            ],
            axis=0,
        )
        at[:, pl.ds(pl.multiple_of(128 * m, 128), 128)] = jnp.concatenate(parts(tile, 3), axis=0)

    def frames_times(x, which=None):
        picked = at[...]
        if which is not None:
            picked = at[:, pl.ds(pl.multiple_of(which * (FH // 2), FH // 2), FH // 2)]
        out = bdot(picked, jnp.concatenate(parts(x, 2), axis=1))
        out = out[:, 0:RANK] + out[:, RANK:]
        return out[0:PX] + (out[PX : 2 * PX] + out[2 * PX :])

    def rows_times(x):
        hi, lo = parts(x, 2)
        return bdot(an[...], jnp.concatenate([hi, hi, lo], axis=0))

    drain(om.at[pl.ds(0, 15)], recv.at[2])
    xs[0] = frames_times(om[...].reshape(FH, RANK))
    push(xs.at[0], xr.at[0], send.at[4], recv.at[4], partner)

    chosen_here = (iota((FH, 128), 0) + half * FH == picks[...]).astype(BF16)
    out = bdot(at[...], chosen_here)
    ss[...] = out[0:PX] + (out[PX : 2 * PX] + out[2 * PX :])
    push(ss, sr, send.at[3], recv.at[3], partner)
    for m in range(NZ // 2):
        tile = at[0 : 2 * PX, 128 * m : 128 * m + 128].astype(F32)
        tile = jnp.concatenate([tile, tile[0:PX]], axis=0)
        an[128 * m : 128 * m + 128, :] = tile.T.astype(BF16)
    drain(xr.at[0], recv.at[4])

    def to_pix(out, got, sem):
        def send_pix(d):
            to = wrap(pix + d, NP)
            push(out.at[to], got.at[pix], send.at[sem], recv.at[sem], (group, to))

        each(RING, send_pix)
        got[pix] = out[pix]

    def all_pix(buffer, sem):
        def send_pix(d):
            push(buffer.at[pix], buffer.at[pix], send.at[sem], recv.at[sem], (group, wrap(pix + d, NP)))

        each(RING, send_pix)

    def total(buffer, sem):
        drain(buffer.at[pl.ds(0, 15)], recv.at[sem])
        value = buffer[0]
        for s in range(1, 16):
            value = value + buffer[s]
        return value

    def tiles_to_z(packed, landed, sem):
        def send_z(d):
            to = wrap(z + d, NZ)
            push(packed.at[to % 8], landed.at[z], send.at[sem], recv.at[sem], (base + to, pix))

        each(RING, send_z)
        landed[z] = packed[z % 8]

    def same_to_z(packed, landed, sem):
        def send_z(d):
            push(packed, landed.at[z], send.at[sem], recv.at[sem], (base + wrap(z + d, NZ), pix))

        each(RING, send_z)
        landed[z] = packed[...]

    basis = xs[0] + xr[0]
    halves = parts(basis, 2)
    stacked = jnp.concatenate([halves[0], halves[0], halves[1]], axis=0)

    def half_of_rows(which):
        y = bdot(an[pl.ds(pl.multiple_of(which * (FH // 2), FH // 2), FH // 2), :], stacked)
        for qq in range(8):
            for k in range(8):
                row = FB * k + 8 * qq
                s1[which, qq, k] = y[row : row + 8, :]

    half_of_rows(1 - c)
    push(s1.at[1 - c], c1, send.at[5], recv.at[5], other_core)
    gram = dot(basis.T, basis)
    for tile in range(NP):
        g1[tile % 2, tile // 2] = gram[8 * tile : 8 * tile + 8, :]
    push(g1.at[1 - c], cg1, send.at[25], recv.at[25], other_core)
    half_of_rows(c)
    drain(c1, recv.at[5])
    drain(cg1, recv.at[25])

    def sum_of_cores(to, into):
        into[to if into is t1 else q, 0:8] = s1[c, to] + c1[to]
        into[to if into is t1 else q, 8] = g1[c, to] + cg1[to]

    def send_eighths(d):
        to = wrap(q + d, 8)
        sum_of_cores(to, t1)
        push(t1.at[to], r1.at[q], send.at[21], recv.at[21], (group, 2 * to + c))

    each(EIGHTHS, send_eighths)
    sum_of_cores(q, r1)
    drain(sr, recv.at[3])
    sel_t[...] = ss[...] + sr[...]
    sel[...] = sel_t[...].T
    drain(r1.at[pl.ds(0, 7)], recv.at[21])
    value = r1[0]
    for s in range(1, 8):
        value = value + r1[s]
    k1[...] = value[0:8]
    kg1[...] = value[8]
    tiles_to_z(k1, zy1, 6)
    same_to_z(kg1, zg1, 17)
    yz[z % 8] = total(zy1, 6)
    for d in (4, -3, 3, -2, 2, -1, 1):
        push(
            yz.at[z % 8], yz.at[z % 8], send.at[7], recv.at[7],
            (base + wrap(z + (d + NZ) % NZ, NZ), pix),
        )
    gf[pix] = total(zg1, 17)
    all_pix(gf, 8)
    drain(yz.at[pl.ds(0, 7)], recv.at[7])
    ours, theirs = pl.ds(8 * c, 8), pl.ds(8 * (1 - c), 8)
    for d in EIGHTHS:
        push(
            yz, yf.at[ours, q], send.at[9], arrive.at[d], (group, 2 * wrap(q + d, 8) + c)
        )
    yf[ours, q] = yz[...]
    push(yf.at[ours, q], yf.at[ours, q], send.at[22], recv.at[22], other_core)
    drain(gf.at[pl.ds(0, NP - 1)], recv.at[8])
    start_factor(work, gf[...].reshape(RANK, RANK))
    eliminate(work, linv, 0, 2)
    for d in EIGHTHS:
        origin = wrap(q + 8 - d, 8)
        drain(yf.at[ours, origin], arrive.at[d])
        push(yf.at[ours, origin], yf.at[ours, origin], send.at[22], recv.at[22], other_core)
    mine = frames_times(yf[ours].reshape(FH // 2, RANK), c)
    eliminate(work, linv, 2, 3)
    drain(yf.at[theirs], recv.at[22])

    xs[1] = mine + frames_times(yf[theirs].reshape(FH // 2, RANK), 1 - c)
    push(xs.at[1], xr.at[1], send.at[10], recv.at[10], partner)
    push(sel_t, near.at[0], send.at[15], recv.at[15], (group, wrap(pix + 1, NP)))
    push(sel_t, near.at[1], send.at[16], recv.at[16], (group, wrap(pix + NP - 1, NP)))
    eliminate(work, linv, 3, 4)
    drain(xr.at[1], recv.at[10])
    basis = dot_nt(xs[1] + xr[1], linv[...])
    across = basis.T
    sg[...] = dot(jnp.where(half == 0, across, sel[...]), basis).reshape(NP, 8, RANK)
    to_pix(sg, rg, 11)
    bs[...] = basis
    push(bs, near.at[2], send.at[23], recv.at[23], (group, wrap(pix + 1, NP)))
    push(bs, near.at[3], send.at[24], recv.at[24], (group, wrap(pix + NP - 1, NP)))
    y = rows_times(basis)
    for owner in range(NP):
        for k in range(8):
            row = FB * (8 * (owner % 2) + k) + 8 * (owner // 2)
            s2[owner, k] = y[row : row + 8, :]
    kg2[...] = total(rg, 11)
    same_to_z(kg2, zg2, 13)
    to_pix(s2, r2, 12)
    place = half * NP + pix
    ft[place] = total(zg2, 13)

    def send_both(d):
        to = wrap(pix + d, NP)
        push(ft.at[place], ft.at[place], send.at[18], recv.at[18], (group, to))
        push(ft.at[place], ft.at[place], send.at[18], recv.at[18], (across_group, to))

    push(ft.at[place], ft.at[place], send.at[18], recv.at[18], partner)
    each(RING, send_both)
    k2[...] = total(r2, 12)
    tiles_to_z(k2, zy2, 19)

    def with_near(own, above, below):
        gap = jnp.zeros((8, 128), F32)
        rows = [own, above[0:PXH], gap, above[PXH:], below, gap]
        return jnp.concatenate(rows, axis=0).T

    for k in range(4):
        drain(near.at[k], recv.at[(15, 16, 23, 24)[k]])
    selx[...] = with_near(sel_t[...], near[0], near[1])
    across_x[...] = with_near(bs[...], near[2], near[3])
    drain(ft.at[pl.ds(0, 2 * NP - 1)], recv.at[18])
    start_factor(work, ft[0:NP].reshape(RANK, RANK))
    eliminate(work, linv, 0, 3)
    fy[pix] = total(zy2, 19)
    all_pix(fy, 20)
    eliminate(work, linv, 3, 4)

    own = dot_nt(ft[pl.ds(NP + 8 * half, 8)].reshape(FB, RANK), linv[...])
    ortho_t = dot(linv[...], across_x[...])
    chosen = selx[pl.ds(pl.multiple_of(FB * half, FB), FB), :] - dot(own, ortho_t)
    shrunk = jnp.where(
        chosen > THRESHOLD,
        chosen - THRESHOLD,
        jnp.where(chosen < -THRESHOLD, chosen + THRESHOLD, 0.0),
    )
    shrunk = shrunk.astype(BF16).astype(F32)
    for t in range(NZ):
        slab[t] = shrunk[4 * t : 4 * t + 4, :]

    def send_slab(d):
        to = wrap(z + d, NZ)
        push(slab.at[to], slabs.at[z], send.at[14], recv.at[14], (base + to, pix))

    each(RING, send_slab)
    slabs[z] = slab[z]
    drain(fy.at[pl.ds(0, NP - 1)], recv.at[20])
    upper = z >= 8
    mine = [jnp.where(upper, fy[2 * k + 1], fy[2 * k]) for k in range(8)]
    coeffs_out[...] = dot_nt(jnp.concatenate(mine, axis=0), linv[...])
    drain(slabs.at[pl.ds(0, NZ - 1)], recv.at[14])

    lane = iota((4, 128), 1)
    first, last = pix == 0, pix == NP - 1
    rows = []
    for part, start in ((0, 80), (1, 0), (0, 0), (0, 40), (1, 40), (1, 80)):
        tiles = [jnp.zeros((4, 128), F32) for _ in range(5)]
        for t in range(NZ):
            at_tile, shift = (PXH * t) // 128, (PXH * t) % 128
            piece = slabs[t, :, 128 * part : 128 * part + 128]
            turn = (shift - start) % 128
            if turn:
                piece = pltpu.roll(piece, turn, 1)
            tiles[at_tile] = jnp.where((lane >= shift) & (lane < shift + PXH), piece, tiles[at_tile])
            if shift + PXH > 128:
                tiles[at_tile + 1] = jnp.where(lane < shift + PXH - 128, piece, tiles[at_tile + 1])
        row = jnp.concatenate(tiles, axis=1)
        if len(rows) < 2:
            row = jnp.where(first, 0.0, row)
        if len(rows) > 3:
            row = jnp.where(last, 0.0, row)
        rows.append(row)
    place_in_row = iota((4, W), 1)
    for b in range(3):
        for k, row in enumerate(rows):
            if b == 0:
                row = jnp.where(place_in_row == 0, 0.0, pltpu.roll(row, 1, 1))
            elif b == 2:
                row = jnp.where(place_in_row == W - 1, 0.0, pltpu.roll(row, W - 1, 1))
            for a in range(3):
                h = k - a
                if 0 <= h < 4:
                    tap = 3 * a + b
                    taps[8 * tap : 8 * tap + 4, W * h : W * h + W] = row
    bias = jnp.concatenate([bias_wide[...]] * 5, axis=1)
    layers = []
    for h in range(4):
        hidden = jnp.dot(
            w1[...], taps[:, W * h : W * h + W].astype(BF16), preferred_element_type=F32
        )
        hidden = jnp.maximum(hidden + bias, 0.0)
        if h == 0:
            hidden = jnp.where(first, 0.0, hidden)
        if h == 3:
            hidden = jnp.where(last, 0.0, hidden)
        layers.append(jnp.dot(w2[...], hidden.astype(BF16), preferred_element_type=F32))
    for r in range(2):
        summed = jnp.broadcast_to(bias_out[...], (4, W))
        for b in range(3):
            part = sum(layers[r + a][8 * (3 * a + b) : 8 * (3 * a + b) + 4, :] for a in range(3))
            if b == 0:
                part = jnp.where(place_in_row == 0, 0.0, pltpu.roll(part, 1, 1))
            elif b == 2:
                part = jnp.where(place_in_row == W - 1, 0.0, pltpu.roll(part, W - 1, 1))
            summed = summed + part
        scores_out[:, W * r : W * r + W] = summed

    @pl.when(carries)
    def _():
        drain(om.at[pl.ds(0, NZ - 1), 0], send.at[0])

    drain(t_buf.at[pl.ds(0, NZ - 1)], send.at[1])
    drain(om.at[pl.ds(0, 15)], send.at[2])
    drain(ss, send.at[3])
    drain(xs.at[0], send.at[4])
    drain(c1, send.at[5])
    drain(cg1, send.at[25])
    drain(r1.at[pl.ds(0, 7)], send.at[21])
    drain(yf.at[theirs], send.at[22])
    drain(zy1.at[pl.ds(0, NZ - 1)], send.at[6])
    drain(yz.at[pl.ds(0, 7)], send.at[7])
    drain(gf.at[pl.ds(0, NP - 1)], send.at[8])
    drain(yf.at[pl.ds(0, 7)], send.at[9])
    drain(xs.at[1], send.at[10])
    drain(sg.at[pl.ds(0, NP - 1)], send.at[11])
    drain(s2.at[pl.ds(0, NP - 1)], send.at[12])
    drain(zg2.at[pl.ds(0, NZ - 1)], send.at[13])
    drain(zg1.at[pl.ds(0, NZ - 1)], send.at[17])
    drain(ft.at[pl.ds(0, 2 * NP - 1)], send.at[18])
    drain(zy2.at[pl.ds(0, NZ - 1)], send.at[19])
    drain(fy.at[pl.ds(0, NP - 1)], send.at[20])
    drain(slab.at[pl.ds(0, NZ - 1)], send.at[14])
    for sem in (15, 16, 23, 24):
        drain(bs, send.at[sem])


def shards(frames, start_basis, picks, conv_in, bias_in, conv_out, bias_out):
    vmem = pltpu.VMEM
    scratch = [
        vmem((FB, 2 * W), F32),
        vmem((1, 128), jnp.int32),
        vmem((1, HID), F32),
        vmem((9, HID), BF16),
        vmem((9, HID), BF16),
        vmem((1, 1), F32),
        vmem((NZ, PXH, 128), F32),
        vmem((NZ, PXH, 128), F32),
        vmem((NZ, 8, 8, RANK), F32),
        vmem((3 * PX, FH), BF16),
        vmem((FH, 3 * PX), BF16),
        vmem((PX, 128), F32),
        vmem((128, PX), F32),
        vmem((2, PX, RANK), F32),
        vmem((2, PX, RANK), F32),
        vmem((PX, 128), F32),
        vmem((PX, 128), F32),
        vmem((2, 8, 8, 8, RANK), F32),
        vmem((2, 8, 8, RANK), F32),
        vmem((8, 8, 8, RANK), F32),
        vmem((8, 8, RANK), F32),
        vmem((8, 9, 8, RANK), F32),
        vmem((8, 9, 8, RANK), F32),
        vmem((8, 8, RANK), F32),
        vmem((NZ, 8, RANK), F32),
        vmem((8, RANK), F32),
        vmem((NZ, 8, RANK), F32),
        vmem((8, 8, RANK), F32),
        vmem((NZ, 8, 8, RANK), F32),
        vmem((NP, 8, RANK), F32),
        vmem((NP, 8, 8, RANK), F32),
        vmem((NP, 8, 8, RANK), F32),
        vmem((8, 8, RANK), F32),
        vmem((NZ, 8, RANK), F32),
        vmem((NP, 8, RANK), F32),
        vmem((NP, 8, RANK), F32),
        vmem((8, RANK), F32),
        vmem((NZ, 8, RANK), F32),
        vmem((2 * NP, 8, RANK), F32),
        vmem((NP, 8, RANK), F32),
        vmem((RANK, 2 * RANK), F32),
        vmem((RANK, RANK), F32),
        vmem((NZ, 4, 256), F32),
        vmem((NZ, 4, 256), F32),
        vmem((4, PX, 128), F32),
        vmem((PX, RANK), F32),
        vmem((128, 256), F32),
        vmem((RANK, 256), F32),
        vmem((72, 4 * W), F32),
        vmem((4 * HID, 72), BF16),
        vmem((72, 4 * HID), BF16),
        vmem((4 * HID, 128), F32),
        pltpu.SemaphoreType.DMA((26,)),
        pltpu.SemaphoreType.DMA((26,)),
        pltpu.SemaphoreType.DMA((7,)),
        pltpu.SemaphoreType.DMA((8,)),
        pltpu.SemaphoreType.DMA((NZ,)),
    ]
    whole = pl.BlockSpec(memory_space=pltpu.VMEM)
    return pl.pallas_call(
        kernel,
        out_shape=(
            jax.ShapeDtypeStruct((FB, RANK), F32),
            jax.ShapeDtypeStruct((4, 2 * W), F32),
        ),
        in_specs=[pl.BlockSpec(memory_space=pltpu.HBM)] * 7,
        out_specs=(whole, whole),
        scratch_shapes=scratch,
        compiler_params=pltpu.CompilerParams(
            collective_id=0, has_side_effects=True, vmem_limit_bytes=64 * 1024 * 1024
        ),
        cost_estimate=pl.CostEstimate(
            flops=1_500_000_000, bytes_accessed=1_000_000, transcendentals=0
        ),
    )(
        frames,
        start_basis,
        picks.reshape(1, 128),
        bias_in.reshape(1, HID),
        conv_in.T,
        conv_out,
        bias_out.reshape(1, 1),
    )


def solution(mesh):
    placed = (P("frame", "pix"), P("frame", None), P(), P(), P(), P(), P())
    return jax.shard_map(
        shards,
        mesh=mesh,
        in_specs=placed,
        out_specs=(P("frame", None), P("frame", "pix")),
        check_vma=False,
    )
```

```python
import jax
import jax.numpy as jnp
from jax import lax
from jax.experimental import pallas as pl
from jax.experimental.pallas import tpu as pltpu
from jax.sharding import PartitionSpec as P

MESH = pl.DeviceIdType.MESH
F32 = jnp.float32
BF16 = jnp.bfloat16

W = 640
RANK = 128
HID = 64
NZ = 16
NP = 16
FB = 64
PXH = 40
PX = 2 * PXH
FH = NZ * FB
THRESHOLD = 0.5


def dot(a, b):
    return lax.dot_general(
        a, b, (((1,), (0,)), ((), ())), precision=lax.Precision.HIGHEST, preferred_element_type=F32
    )


def dot_nt(a, b):
    return lax.dot_general(
        a, b, (((1,), (1,)), ((), ())), precision=lax.Precision.HIGHEST, preferred_element_type=F32
    )


def iota(shape, dim):
    return lax.broadcasted_iota(jnp.int32, shape, dim)


BLOCK = 32


def start_factor(work, gram):
    diagonal = iota((RANK, RANK), 0) == iota((RANK, RANK), 1)
    own = jnp.where(diagonal, gram, 0.0)
    by_row = 1.0 / jnp.sqrt(jnp.sum(own, axis=1, keepdims=True))
    by_column = 1.0 / jnp.sqrt(jnp.sum(own, axis=0, keepdims=True))
    work[:, 0:RANK] = gram * by_row * by_column
    work[:, RANK : 2 * RANK] = jnp.where(diagonal, by_column, 0.0)


def eliminate(work, result, first, last):
    tiles = BLOCK // 8
    row_in_tile = iota((8, 128), 0)

    def one(number, carry):
        left = [work[8 * t : 8 * t + 8, 0:RANK] for t in range(tiles)]
        right = [work[8 * t : 8 * t + 8, RANK:] for t in range(tiles)]
        columns = [
            [jnp.broadcast_to(left[t][:, m : m + 1], (8, 128)) for t in range(tiles)]
            for m in range(BLOCK)
        ]
        pivots = []
        for j in range(0, BLOCK, 2):
            t0, r0 = j // 8, j % 8

            def row_of(tile, r):
                return jnp.broadcast_to(tile[r : r + 1, :], (8, 128))

            one_, cross = row_of(columns[j][t0], r0), row_of(columns[j + 1][t0], r0)
            two = row_of(columns[j + 1][t0], r0 + 1)
            det = one_ * two - cross * cross
            over_one = 1.0 / one_
            over_two = one_ * (1.0 / det)
            link = cross * over_one
            pivots += [one_, det * over_one]
            first, second = {}, {}
            for t in range(t0, tiles):
                first[t] = columns[j][t] * over_one
                second[t] = (columns[j + 1][t] - link * columns[j][t]) * over_two
            first[t0] = jnp.where(row_in_tile > r0 + 1, first[t0], 0.0)
            second[t0] = jnp.where(row_in_tile > r0 + 1, second[t0], 0.0)
            for m in range(j + 2, BLOCK):
                upper = row_of(columns[m][t0], r0)
                lower = row_of(columns[m][t0], r0 + 1) - link * upper
                for t in range(t0, tiles):
                    columns[m][t] = columns[m][t] - (first[t] * upper + second[t] * lower)
            for side in (left, right):
                upper = row_of(side[t0], r0)
                lower = row_of(side[t0], r0 + 1) - link * upper
                for t in range(t0, tiles):
                    side[t] = side[t] - (first[t] * upper + second[t] * lower)
                side[t0] = jnp.where(row_in_tile == r0 + 1, lower, side[t0])
        for t in range(tiles):
            own = pivots[8 * t]
            for r in range(1, 8):
                own = jnp.where(row_in_tile == r, pivots[8 * t + r], own)
            scale = 1.0 / jnp.sqrt(own)
            left[t] = left[t] * scale
            right[t] = right[t] * scale
        left = jnp.concatenate(left, axis=0)
        right = jnp.concatenate(right, axis=0)
        result[pl.ds(pl.multiple_of(number * BLOCK, BLOCK), BLOCK), :] = right

        @pl.when(number < RANK // BLOCK - 1)
        def _():
            across = left.T[BLOCK:, :]
            rest = work[BLOCK:, 0:RANK] - dot(across, left)
            work[0 : RANK - BLOCK, 0:RANK] = pltpu.roll(rest, RANK - BLOCK, 1)
            work[0 : RANK - BLOCK, RANK:] = work[BLOCK:, RANK:] - dot(across, right)

        return carry

    lax.fori_loop(first, last, one, 0)


def push(src, dst, send, recv, device):
    pltpu.make_async_remote_copy(
        src_ref=src, dst_ref=dst, send_sem=send, recv_sem=recv,
        device_id={"frame": device[0], "pix": device[1]}, device_id_type=MESH,
    ).start()


def parts(x, count):
    out = []
    for _ in range(count):
        out.append(x.astype(BF16))
        x = x - out[-1].astype(F32)
    return out


def bdot(a, b):
    return jnp.dot(a, b, preferred_element_type=F32)


RING = (8, 7, 9, 6, 10, 5, 11, 4, 12, 3, 13, 2, 14, 1, 15)
EIGHTHS = (4, 2, 6, 5, 3, 7, 1)


def each(distances, send):
    for d in distances:
        send(d)


def drain(ref, sem):
    pltpu.make_async_copy(ref, ref, sem).wait()


def kernel(
    frames_hbm, basis0, picks_hbm, bias_in_hbm, conv_in_hbm, conv_out_hbm, bias_out_hbm,
    coeffs_out, scores_out,
    frames, picks, bias_in, conv_in, conv_out, bias_out, t_buf, r_buf, om, at, an, sel_t, sel, xs, xr, ss, sr,
    s1, g1, c1, cg1, t1, r1, k1, zy1, kg1, zg1, yz, yf, gf,
    s2, r2, k2, zy2, sg, rg, kg2, zg2, ft, fy,
    work, linv, slab, slabs, near, bs, selx, across_x, taps, w1, w2, bias_wide,
    send, recv, load, arrive, came,
):
    group = lax.axis_index("frame")
    pix = lax.axis_index("pix")
    half = group // NZ
    z = group % NZ
    base = half * NZ
    q = pix // 2
    c = pix % 2
    fetch = pltpu.make_async_copy(frames_hbm, frames, load.at[0])
    fetch.start()
    small = [
        pltpu.make_async_copy(src, dst, load.at[2 + n])
        for n, (src, dst) in enumerate(
            (
                (picks_hbm, picks),
                (bias_in_hbm, bias_in),
                (conv_in_hbm, conv_in),
                (conv_out_hbm, conv_out),
                (bias_out_hbm, bias_out),
            )
        )
    ]
    for copy in small:
        copy.start()

    across_group = (1 - half) * NZ + z
    partner = (across_group, pix)
    other_core = (group, 2 * q + 1 - c)
    wrap = lax.rem

    barrier = pltpu.get_barrier_semaphore()

    def greet(d):
        to = wrap(pix + d, NP)
        for frame, at_pix in ((base + wrap(z + d, NZ), pix), (group, to), (across_group, to)):
            pl.semaphore_signal(
                barrier, inc=1, device_id={"frame": frame, "pix": at_pix}, device_id_type=MESH
            )

    each(RING, greet)
    pl.semaphore_signal(
        barrier, inc=1, device_id={"frame": across_group, "pix": pix}, device_id_type=MESH
    )

    fetch.wait()
    both = jnp.concatenate([frames[:, 0:W], frames[:, W : 2 * W]], axis=0)
    for t in range(5):
        tile = both[:, 128 * t : 128 * t + 128].T
        for lo in range(128 * t, 128 * t + 128, 8):
            t_buf[lo // PXH, lo % PXH : lo % PXH + 8, :] = tile[lo - 128 * t : lo - 128 * t + 8, :]

    pl.semaphore_wait(barrier, 46)

    eighth = pl.multiple_of(q * 8, 8)

    def send_basis(d):
        push(
            basis0.at[pl.ds(eighth, 8)], om.at[z, q], send.at[0], recv.at[0],
            (base + wrap(z + d, NZ), pix),
        )

    def send_frames(d):
        to = wrap(z + d, NZ)
        push(t_buf.at[to], r_buf.at[z], send.at[1], came.at[z], (base + to, pix))

    carries = c == z // 8

    @pl.when(carries)
    def _():
        each(RING, send_basis)

    each(RING[:2], send_frames)

    @pl.when(carries)
    def _():
        own_part = pltpu.make_async_copy(basis0.at[pl.ds(eighth, 8)], om.at[z, q], load.at[1])
        own_part.start()
        own_part.wait()

    r_buf[z] = t_buf[z]

    for copy in small:
        copy.wait()
    up = (iota((4 * HID, HID), 0) % HID == iota((4 * HID, HID), 1))
    wide = (iota((9, 72), 1) // 8 == iota((9, 72), 0))
    same = iota((4 * HID, 72), 0) // HID == iota((4 * HID, 72), 1) % 8
    spread = lax.dot_general(
        conv_in[...], wide.astype(BF16), (((0,), (0,)), ((), ())), preferred_element_type=F32
    ).astype(BF16)
    spread = jnp.dot(up.astype(BF16), spread, preferred_element_type=F32)
    w1[...] = jnp.where(same, spread, 0.0).astype(BF16)
    tall = (iota((72, 9), 0) // 8 == iota((72, 9), 1))
    over = (iota((HID, 4 * HID), 1) % HID == iota((HID, 4 * HID), 0))
    same = iota((72, 4 * HID), 1) // HID == iota((72, 4 * HID), 0) % 8
    spread = jnp.dot(tall.astype(BF16), conv_out[...], preferred_element_type=F32).astype(BF16)
    spread = jnp.dot(spread, over.astype(BF16), preferred_element_type=F32)
    w2[...] = jnp.where(same, spread, 0.0).astype(BF16)
    bias_wide[...] = dot_nt(up.astype(F32), jnp.broadcast_to(bias_in[...], (128, HID)))
    taps[...] = jnp.zeros_like(taps)

    @pl.when(carries)
    def _():
        drain(om.at[pl.ds(0, 7), 0], recv.at[0])

    @pl.when(c != z // 8)
    def _():
        drain(om.at[pl.ds(0, 8), 0], recv.at[0])

    lower_z = pl.ds(8 * c, 8)

    def spread_basis(d):
        push(
            om.at[lower_z, q], om.at[lower_z, q], send.at[2], recv.at[2], (group, wrap(pix + d, NP))
        )

    for n, d in enumerate(RING):
        spread_basis(d)
        each(RING[2 + n : 3 + n], send_frames)

    low = iota((PXH, 128), 1) < FB
    for k in (4, 3, 5, 2, 6, 1, 7, 0):
        m = wrap(z // 2 + k, NZ // 2)
        if k:
            drain(r_buf.at[2 * m], came.at[2 * m])
            drain(r_buf.at[2 * m + 1], came.at[2 * m + 1])
        else:
            other = 2 * m + 1 - z % 2
            drain(r_buf.at[other], came.at[other])
        first, second = r_buf[2 * m], r_buf[2 * m + 1]
        tile = jnp.concatenate(
            [
                jnp.where(low, first, pltpu.roll(second, FB, 1)),
                jnp.where(low, pltpu.roll(first, FB, 1), second),
            ],
            axis=0,
        )
        at[:, pl.ds(pl.multiple_of(128 * m, 128), 128)] = jnp.concatenate(parts(tile, 3), axis=0)

    def frames_times(x, which=None):
        picked = at[...]
        if which is not None:
            picked = at[:, pl.ds(pl.multiple_of(which * (FH // 2), FH // 2), FH // 2)]
        out = bdot(picked, jnp.concatenate(parts(x, 2), axis=1))
        out = out[:, 0:RANK] + out[:, RANK:]
        return out[0:PX] + (out[PX : 2 * PX] + out[2 * PX :])

    def rows_times(x):
        hi, lo = parts(x, 2)
        return bdot(an[...], jnp.concatenate([hi, hi, lo], axis=0))

    drain(om.at[pl.ds(0, 15)], recv.at[2])
    xs[0] = frames_times(om[...].reshape(FH, RANK))
    push(xs.at[0], xr.at[0], send.at[4], recv.at[4], partner)

    chosen_here = (iota((FH, 128), 0) + half * FH == picks[...]).astype(BF16)
    out = bdot(at[...], chosen_here)
    ss[...] = out[0:PX] + (out[PX : 2 * PX] + out[2 * PX :])
    push(ss, sr, send.at[3], recv.at[3], partner)
    for m in range(NZ // 2):
        tile = at[0 : 2 * PX, 128 * m : 128 * m + 128].astype(F32)
        tile = jnp.concatenate([tile, tile[0:PX]], axis=0)
        an[128 * m : 128 * m + 128, :] = tile.T.astype(BF16)
    drain(xr.at[0], recv.at[4])

    def to_pix(out, got, sem):
        def send_pix(d):
            to = wrap(pix + d, NP)
            push(out.at[to], got.at[pix], send.at[sem], recv.at[sem], (group, to))

        each(RING, send_pix)
        got[pix] = out[pix]

    def all_pix(buffer, sem):
        def send_pix(d):
            push(buffer.at[pix], buffer.at[pix], send.at[sem], recv.at[sem], (group, wrap(pix + d, NP)))

        each(RING, send_pix)

    def total(buffer, sem):
        drain(buffer.at[pl.ds(0, 15)], recv.at[sem])
        value = buffer[0]
        for s in range(1, 16):
            value = value + buffer[s]
        return value

    def tiles_to_z(packed, landed, sem):
        def send_z(d):
            to = wrap(z + d, NZ)
            push(packed.at[to % 8], landed.at[z], send.at[sem], recv.at[sem], (base + to, pix))

        each(RING, send_z)
        landed[z] = packed[z % 8]

    def same_to_z(packed, landed, sem):
        def send_z(d):
            push(packed, landed.at[z], send.at[sem], recv.at[sem], (base + wrap(z + d, NZ), pix))

        each(RING, send_z)
        landed[z] = packed[...]

    basis = xs[0] + xr[0]
    halves = parts(basis, 2)
    stacked = jnp.concatenate([halves[0], halves[0], halves[1]], axis=0)

    def half_of_rows(which):
        y = bdot(an[pl.ds(pl.multiple_of(which * (FH // 2), FH // 2), FH // 2), :], stacked)
        for qq in range(8):
            for k in range(8):
                row = FB * k + 8 * qq
                s1[which, qq, k] = y[row : row + 8, :]

    half_of_rows(1 - c)
    push(s1.at[1 - c], c1, send.at[5], recv.at[5], other_core)
    gram = dot(basis.T, basis)
    for tile in range(NP):
        g1[tile % 2, tile // 2] = gram[8 * tile : 8 * tile + 8, :]
    push(g1.at[1 - c], cg1, send.at[25], recv.at[25], other_core)
    half_of_rows(c)
    drain(c1, recv.at[5])
    drain(cg1, recv.at[25])

    def sum_of_cores(to, into):
        into[to if into is t1 else q, 0:8] = s1[c, to] + c1[to]
        into[to if into is t1 else q, 8] = g1[c, to] + cg1[to]

    def send_eighths(d):
        to = wrap(q + d, 8)
        sum_of_cores(to, t1)
        push(t1.at[to], r1.at[q], send.at[21], recv.at[21], (group, 2 * to + c))

    each(EIGHTHS, send_eighths)
    sum_of_cores(q, r1)
    drain(sr, recv.at[3])
    sel_t[...] = ss[...] + sr[...]
    sel[...] = sel_t[...].T
    drain(r1.at[pl.ds(0, 7)], recv.at[21])
    value = r1[0]
    for s in range(1, 8):
        value = value + r1[s]
    k1[...] = value[0:8]
    kg1[...] = value[8]
    tiles_to_z(k1, zy1, 6)
    same_to_z(kg1, zg1, 17)
    yz[z % 8] = total(zy1, 6)
    for d in (4, -3, 3, -2, 2, -1, 1):
        push(
            yz.at[z % 8], yz.at[z % 8], send.at[7], recv.at[7],
            (base + wrap(z + (d + NZ) % NZ, NZ), pix),
        )
    gf[pix] = total(zg1, 17)
    all_pix(gf, 8)
    drain(yz.at[pl.ds(0, 7)], recv.at[7])
    ours, theirs = pl.ds(8 * c, 8), pl.ds(8 * (1 - c), 8)
    for d in EIGHTHS:
        push(
            yz, yf.at[ours, q], send.at[9], arrive.at[d], (group, 2 * wrap(q + d, 8) + c)
        )
    yf[ours, q] = yz[...]
    push(yf.at[ours, q], yf.at[ours, q], send.at[22], recv.at[22], other_core)
    drain(gf.at[pl.ds(0, NP - 1)], recv.at[8])
    start_factor(work, gf[...].reshape(RANK, RANK))
    eliminate(work, linv, 0, 2)
    for d in EIGHTHS:
        origin = wrap(q + 8 - d, 8)
        drain(yf.at[ours, origin], arrive.at[d])
        push(yf.at[ours, origin], yf.at[ours, origin], send.at[22], recv.at[22], other_core)
    mine = frames_times(yf[ours].reshape(FH // 2, RANK), c)
    eliminate(work, linv, 2, 3)
    drain(yf.at[theirs], recv.at[22])

    xs[1] = mine + frames_times(yf[theirs].reshape(FH // 2, RANK), 1 - c)
    push(xs.at[1], xr.at[1], send.at[10], recv.at[10], partner)
    push(sel_t, near.at[0], send.at[15], recv.at[15], (group, wrap(pix + 1, NP)))
    push(sel_t, near.at[1], send.at[16], recv.at[16], (group, wrap(pix + NP - 1, NP)))
    eliminate(work, linv, 3, 4)
    drain(xr.at[1], recv.at[10])
    basis = dot_nt(xs[1] + xr[1], linv[...])
    across = basis.T
    sg[...] = dot(jnp.where(half == 0, across, sel[...]), basis).reshape(NP, 8, RANK)
    to_pix(sg, rg, 11)
    bs[...] = basis
    push(bs, near.at[2], send.at[23], recv.at[23], (group, wrap(pix + 1, NP)))
    push(bs, near.at[3], send.at[24], recv.at[24], (group, wrap(pix + NP - 1, NP)))
    y = rows_times(basis)
    for owner in range(NP):
        for k in range(8):
            row = FB * (8 * (owner % 2) + k) + 8 * (owner // 2)
            s2[owner, k] = y[row : row + 8, :]
    kg2[...] = total(rg, 11)
    same_to_z(kg2, zg2, 13)
    to_pix(s2, r2, 12)
    place = half * NP + pix
    ft[place] = total(zg2, 13)

    def send_both(d):
        to = wrap(pix + d, NP)
        push(ft.at[place], ft.at[place], send.at[18], recv.at[18], (across_group, to))
        push(ft.at[place], ft.at[place], send.at[18], recv.at[18], (group, to))

    push(ft.at[place], ft.at[place], send.at[18], recv.at[18], partner)
    each(RING, send_both)
    k2[...] = total(r2, 12)
    tiles_to_z(k2, zy2, 19)

    def with_near(own, above, below):
        gap = jnp.zeros((8, 128), F32)
        rows = [own, above[0:PXH], gap, above[PXH:], below, gap]
        return jnp.concatenate(rows, axis=0).T

    for k in range(4):
        drain(near.at[k], recv.at[(15, 16, 23, 24)[k]])
    selx[...] = with_near(sel_t[...], near[0], near[1])
    across_x[...] = with_near(bs[...], near[2], near[3])
    drain(ft.at[pl.ds(0, 2 * NP - 1)], recv.at[18])
    start_factor(work, ft[0:NP].reshape(RANK, RANK))
    eliminate(work, linv, 0, 3)
    fy[pix] = total(zy2, 19)
    all_pix(fy, 20)
    eliminate(work, linv, 3, 4)

    own = dot_nt(ft[pl.ds(NP + 8 * half, 8)].reshape(FB, RANK), linv[...])
    ortho_t = dot(linv[...], across_x[...])
    chosen = selx[pl.ds(pl.multiple_of(FB * half, FB), FB), :] - dot(own, ortho_t)
    shrunk = jnp.where(
        chosen > THRESHOLD,
        chosen - THRESHOLD,
        jnp.where(chosen < -THRESHOLD, chosen + THRESHOLD, 0.0),
    )
    shrunk = shrunk.astype(BF16).astype(F32)
    for t in range(NZ):
        slab[t] = shrunk[4 * t : 4 * t + 4, :]

    def send_slab(d):
        to = wrap(z + d, NZ)
        push(slab.at[to], slabs.at[z], send.at[14], recv.at[14], (base + to, pix))

    each(RING, send_slab)
    slabs[z] = slab[z]
    drain(fy.at[pl.ds(0, NP - 1)], recv.at[20])
    upper = z >= 8
    mine = [jnp.where(upper, fy[2 * k + 1], fy[2 * k]) for k in range(8)]
    coeffs_out[...] = dot_nt(jnp.concatenate(mine, axis=0), linv[...])
    drain(slabs.at[pl.ds(0, NZ - 1)], recv.at[14])

    lane = iota((4, 128), 1)
    first, last = pix == 0, pix == NP - 1
    rows = []
    for part, start in ((0, 80), (1, 0), (0, 0), (0, 40), (1, 40), (1, 80)):
        tiles = [jnp.zeros((4, 128), F32) for _ in range(5)]
        for t in range(NZ):
            at_tile, shift = (PXH * t) // 128, (PXH * t) % 128
            piece = slabs[t, :, 128 * part : 128 * part + 128]
            turn = (shift - start) % 128
            if turn:
                piece = pltpu.roll(piece, turn, 1)
            tiles[at_tile] = jnp.where((lane >= shift) & (lane < shift + PXH), piece, tiles[at_tile])
            if shift + PXH > 128:
                tiles[at_tile + 1] = jnp.where(lane < shift + PXH - 128, piece, tiles[at_tile + 1])
        row = jnp.concatenate(tiles, axis=1)
        if len(rows) < 2:
            row = jnp.where(first, 0.0, row)
        if len(rows) > 3:
            row = jnp.where(last, 0.0, row)
        rows.append(row)
    place_in_row = iota((4, W), 1)
    for b in range(3):
        for k, row in enumerate(rows):
            if b == 0:
                row = jnp.where(place_in_row == 0, 0.0, pltpu.roll(row, 1, 1))
            elif b == 2:
                row = jnp.where(place_in_row == W - 1, 0.0, pltpu.roll(row, W - 1, 1))
            for a in range(3):
                h = k - a
                if 0 <= h < 4:
                    tap = 3 * a + b
                    taps[8 * tap : 8 * tap + 4, W * h : W * h + W] = row
    bias = jnp.concatenate([bias_wide[...]] * 5, axis=1)
    layers = []
    for h in range(4):
        hidden = jnp.dot(
            w1[...], taps[:, W * h : W * h + W].astype(BF16), preferred_element_type=F32
        )
        hidden = jnp.maximum(hidden + bias, 0.0)
        if h == 0:
            hidden = jnp.where(first, 0.0, hidden)
        if h == 3:
            hidden = jnp.where(last, 0.0, hidden)
        layers.append(jnp.dot(w2[...], hidden.astype(BF16), preferred_element_type=F32))
    for r in range(2):
        summed = jnp.broadcast_to(bias_out[...], (4, W))
        for b in range(3):
            part = sum(layers[r + a][8 * (3 * a + b) : 8 * (3 * a + b) + 4, :] for a in range(3))
            if b == 0:
                part = jnp.where(place_in_row == 0, 0.0, pltpu.roll(part, 1, 1))
            elif b == 2:
                part = jnp.where(place_in_row == W - 1, 0.0, pltpu.roll(part, W - 1, 1))
            summed = summed + part
        scores_out[:, W * r : W * r + W] = summed

    @pl.when(carries)
    def _():
        drain(om.at[pl.ds(0, NZ - 1), 0], send.at[0])

    drain(t_buf.at[pl.ds(0, NZ - 1)], send.at[1])
    drain(om.at[pl.ds(0, 15)], send.at[2])
    drain(ss, send.at[3])
    drain(xs.at[0], send.at[4])
    drain(c1, send.at[5])
    drain(cg1, send.at[25])
    drain(r1.at[pl.ds(0, 7)], send.at[21])
    drain(yf.at[theirs], send.at[22])
    drain(zy1.at[pl.ds(0, NZ - 1)], send.at[6])
    drain(yz.at[pl.ds(0, 7)], send.at[7])
    drain(gf.at[pl.ds(0, NP - 1)], send.at[8])
    drain(yf.at[pl.ds(0, 7)], send.at[9])
    drain(xs.at[1], send.at[10])
    drain(sg.at[pl.ds(0, NP - 1)], send.at[11])
    drain(s2.at[pl.ds(0, NP - 1)], send.at[12])
    drain(zg2.at[pl.ds(0, NZ - 1)], send.at[13])
    drain(zg1.at[pl.ds(0, NZ - 1)], send.at[17])
    drain(ft.at[pl.ds(0, 2 * NP - 1)], send.at[18])
    drain(zy2.at[pl.ds(0, NZ - 1)], send.at[19])
    drain(fy.at[pl.ds(0, NP - 1)], send.at[20])
    drain(slab.at[pl.ds(0, NZ - 1)], send.at[14])
    for sem in (15, 16, 23, 24):
        drain(bs, send.at[sem])


def shards(frames, start_basis, picks, conv_in, bias_in, conv_out, bias_out):
    vmem = pltpu.VMEM
    scratch = [
        vmem((FB, 2 * W), F32),
        vmem((1, 128), jnp.int32),
        vmem((1, HID), F32),
        vmem((9, HID), BF16),
        vmem((9, HID), BF16),
        vmem((1, 1), F32),
        vmem((NZ, PXH, 128), F32),
        vmem((NZ, PXH, 128), F32),
        vmem((NZ, 8, 8, RANK), F32),
        vmem((3 * PX, FH), BF16),
        vmem((FH, 3 * PX), BF16),
        vmem((PX, 128), F32),
        vmem((128, PX), F32),
        vmem((2, PX, RANK), F32),
        vmem((2, PX, RANK), F32),
        vmem((PX, 128), F32),
        vmem((PX, 128), F32),
        vmem((2, 8, 8, 8, RANK), F32),
        vmem((2, 8, 8, RANK), F32),
        vmem((8, 8, 8, RANK), F32),
        vmem((8, 8, RANK), F32),
        vmem((8, 9, 8, RANK), F32),
        vmem((8, 9, 8, RANK), F32),
        vmem((8, 8, RANK), F32),
        vmem((NZ, 8, RANK), F32),
        vmem((8, RANK), F32),
        vmem((NZ, 8, RANK), F32),
        vmem((8, 8, RANK), F32),
        vmem((NZ, 8, 8, RANK), F32),
        vmem((NP, 8, RANK), F32),
        vmem((NP, 8, 8, RANK), F32),
        vmem((NP, 8, 8, RANK), F32),
        vmem((8, 8, RANK), F32),
        vmem((NZ, 8, RANK), F32),
        vmem((NP, 8, RANK), F32),
        vmem((NP, 8, RANK), F32),
        vmem((8, RANK), F32),
        vmem((NZ, 8, RANK), F32),
        vmem((2 * NP, 8, RANK), F32),
        vmem((NP, 8, RANK), F32),
        vmem((RANK, 2 * RANK), F32),
        vmem((RANK, RANK), F32),
        vmem((NZ, 4, 256), F32),
        vmem((NZ, 4, 256), F32),
        vmem((4, PX, 128), F32),
        vmem((PX, RANK), F32),
        vmem((128, 256), F32),
        vmem((RANK, 256), F32),
        vmem((72, 4 * W), F32),
        vmem((4 * HID, 72), BF16),
        vmem((72, 4 * HID), BF16),
        vmem((4 * HID, 128), F32),
        pltpu.SemaphoreType.DMA((26,)),
        pltpu.SemaphoreType.DMA((26,)),
        pltpu.SemaphoreType.DMA((7,)),
        pltpu.SemaphoreType.DMA((8,)),
        pltpu.SemaphoreType.DMA((NZ,)),
    ]
    whole = pl.BlockSpec(memory_space=pltpu.VMEM)
    return pl.pallas_call(
        kernel,
        out_shape=(
            jax.ShapeDtypeStruct((FB, RANK), F32),
            jax.ShapeDtypeStruct((4, 2 * W), F32),
        ),
        in_specs=[pl.BlockSpec(memory_space=pltpu.HBM)] * 7,
        out_specs=(whole, whole),
        scratch_shapes=scratch,
        compiler_params=pltpu.CompilerParams(
            collective_id=0, has_side_effects=True, vmem_limit_bytes=64 * 1024 * 1024
        ),
        cost_estimate=pl.CostEstimate(
            flops=1_500_000_000, bytes_accessed=1_000_000, transcendentals=0
        ),
    )(
        frames,
        start_basis,
        picks.reshape(1, 128),
        bias_in.reshape(1, HID),
        conv_in.T,
        conv_out,
        bias_out.reshape(1, 1),
    )


def solution(mesh):
    placed = (P("frame", "pix"), P("frame", None), P(), P(), P(), P(), P())
    return jax.shard_map(
        shards,
        mesh=mesh,
        in_specs=placed,
        out_specs=(P("frame", None), P("frame", "pix")),
        check_vma=False,
    )
```
